256 devices in a mesh: dp: 16 (over y, x_hi, core), mem: 16 (over x_lo, z).
Axes of the slice: x: 4 (x_hi: 2, x_lo: 2; x = x_hi * 2 + x_lo), y: 4, z: 8, core: 2. Of those that a mesh axis runs over, the one named last changes fastest.
Arguments:
- queries: bfloat16 [4096, 4096], P(('dp', 'mem')), may hold values from -8 to 8
- memory: bfloat16 [32768, 4096], P('mem'), may hold values from -7 to 7
- log_scale: float32 [1], replicated, may hold values from 1.0986 to 1.6094
- labels: int32 [4096], P('dp'), may hold values from 0 to 32767, as said below
- valid: int32 [32768], P('mem'), may hold values from 0 to 1
- cotangent: float32 [4096], P('dp'), may hold values from -20 to 20
Outputs:
- grad_queries: bfloat16 [4096, 4096], P(('dp', 'mem'))
- scale_grad: float32 [1], replicated
The draws below stay inside these ranges and needn't reach their ends.
Inputs may be any that keep to these rules, and one draw needn't show every extreme that they name: `labels`: every label names a memory row whose valid entry is 1.
All inputs are finite; a program needn't handle non-finite values.
Results may differ from the reference program's by a relative error of at most 0.022.
Values may be sent and summed in bfloat16 or wider, within the bound.
No kernel may reach another device: no remote copies, remote signals or barrier semaphores. Data moves between devices by JAX's collectives and lax.ppermute only.
A program may use at most 64 MiB of HBM per device.

```python
import jax
import jax.numpy as jnp
from jax import lax

D = 4096
Q_DEV = 16
MEM_DEV = 2048
QUERIES = 4096
ROWS = 32768
N_MEM = 16


def pairs(key):
    first = jax.random.randint(jax.random.fold_in(key, 11), (8,), 0, ROWS).astype(jnp.int32)
    step = jax.random.randint(jax.random.fold_in(key, 12), (8,), 1, ROWS).astype(jnp.int32)
    return (first, (first + step) % ROWS)


def bank(key):
    base = jnp.clip(jax.random.normal(jax.random.fold_in(key, 21), (ROWS, D), jnp.float32), -6.0, 6.0)
    first, second = pairs(key)
    noise = jnp.clip(jax.random.normal(jax.random.fold_in(key, 22), (8, D), jnp.float32), -6.0, 6.0)
    return base.at[second].set(0.99 * base[first] + 0.14 * noise)


def draw_memory(key, part):
    return bank(key).astype(jnp.bfloat16)


def draw_queries(key, part):
    key = jax.random.fold_in(key, 2)
    base = jnp.clip(jax.random.normal(key, (QUERIES, D), jnp.float32), -6.0, 6.0) * D ** (-0.5)
    return base.astype(jnp.bfloat16)


def draw_labels(key, part):
    key = jax.random.fold_in(key, 3)
    return jax.random.randint(key, (QUERIES,), 0, ROWS).astype(jnp.int32)


def draw_valid(key, part):
    labels = draw_labels(key, part)
    first, second = pairs(key)
    key = jax.random.fold_in(key, 4)
    live = (jax.random.randint(key, (ROWS,), 0, 5) > 0).astype(jnp.int32)
    return live.at[labels].set(1).at[first].set(1).at[second].set(1)


def draw_cotangent(key, part):
    key = jax.random.fold_in(key, 5)
    rise = 1.0 + 2.0 * jnp.arange(QUERIES, dtype=jnp.float32) / (QUERIES - 1)
    base = jnp.clip(jax.random.normal(key, (QUERIES,), jnp.float32), -5.0, 5.0)
    return base * rise


def setup_inputs(seed: int = 0) -> dict:
    keys = jax.random.split(jax.random.key(seed), 7)
    return {
        "queries": draw_queries(jax.random.fold_in(keys[6], 71), 0),
        "memory": draw_memory(jax.random.fold_in(keys[6], 71), 0),
        "log_scale": jnp.clip(jax.random.uniform(keys[2], (1,), jnp.float32, 1.0986, 1.6094), 1.0986, 1.6094),
        "labels": draw_labels(jax.random.fold_in(keys[6], 71), 0),
        "valid": draw_valid(jax.random.fold_in(keys[6], 71), 0),
        "cotangent": draw_cotangent(jax.random.fold_in(keys[6], 71), 0),
    }


def reference(queries, memory, log_scale, labels, valid, cotangent):
    scale = jnp.exp(log_scale[0])
    live = valid > 0
    group = Q_DEV * N_MEM
    nblocks = QUERIES // group
    columns = jnp.arange(ROWS, dtype=jnp.int32)

    def one_block(items):
        query_block, label_block, grad_block = items
        raw = lax.dot_general(query_block, memory, (((1,), (1,)), ((), ())), preferred_element_type=jnp.float32)
        logits = jnp.where(live[None, :], scale * raw, jnp.float32(-1e30))
        top = jnp.max(logits, axis=1)
        expo = jnp.exp(logits - top[:, None])
        total = jnp.sum(expo, axis=1)
        hit = (label_block[:, None] == columns[None, :]).astype(jnp.float32)
        weight = expo / total[:, None] - hit
        scale_part = jnp.sum(grad_block * jnp.sum(weight * raw, axis=1))
        weight_half = weight.astype(jnp.bfloat16)
        summed = jnp.zeros((group, D), jnp.float32)
        for blk in range(N_MEM):
            piece = jnp.dot(weight_half[:, blk * MEM_DEV:(blk + 1) * MEM_DEV], memory[blk * MEM_DEV:(blk + 1) * MEM_DEV], preferred_element_type=jnp.float32)
            rounded = lax.optimization_barrier(piece.astype(jnp.bfloat16))
            summed = summed + rounded.astype(jnp.float32)
        grads = (scale * grad_block[:, None] * summed).astype(jnp.bfloat16)
        return grads, scale_part

    grads, parts = lax.map(one_block, (queries.reshape(nblocks, group, D), labels.reshape(nblocks, group), cotangent.reshape(nblocks, group)))
    scale_grad = (scale * jnp.sum(parts) / QUERIES).reshape(1)
    return grads.reshape(QUERIES, D), scale_grad
```

```python
import jax
import jax.numpy as jnp
from jax import lax
from jax.experimental import pallas as pl
from jax.experimental.pallas import tpu as pltpu
from jax.sharding import PartitionSpec as P

AXES = ("dp", "mem")
NEG = -1e30
VMEM = 48 * 1024 * 1024
BLK = 256
COLS = 512


def table(move):
    pairs = []
    for y in range(4):
        for x in range(4):
            for c in range(2):
                for z in range(8):
                    index = lambda y, x, c, z: (((y * 2 + x // 2) * 2 + c) * 2 + x % 2) * 8 + z
                    pairs.append((index(y, x, c, z), index(*move(y, x, c, z))))
    return pairs


def along_z(k):
    return table(lambda y, x, c, z: (y, x, c, (z + k) % 8))


def partner_of(x, c):
    if c == 0:
        return x ^ 1
    return (x + 1) % 4 if x % 2 else (x - 1) % 4


PARTNER = table(lambda y, x, c, z: (y, partner_of(x, c), c, z))
CORE = table(lambda y, x, c, z: (y, x, 1 - c, z))
X1 = table(lambda y, x, c, z: (y, x ^ 1, c, z))
X2 = table(lambda y, x, c, z: (y, x ^ 2, c, z))
Y1 = table(lambda y, x, c, z: (y ^ 1, x, c, z))
Y2 = table(lambda y, x, c, z: (y ^ 2, x, c, z))


def send(x, pairs):
    return lax.ppermute(x, AXES, pairs)


def logits_kernel(scale_ref, shift_ref, q_ref, mem_ref, lab_ref, valid_ref, e_ref, stat_ref, l_scr, m_scr, ll_scr):
    i = pl.program_id(0)

    @pl.when(i == 0)
    def _():
        m_scr[...] = jnp.full_like(m_scr, NEG)
        ll_scr[...] = jnp.zeros_like(ll_scr)

    raw = lax.dot_general(
        q_ref[...], mem_ref[...], (((1,), (1,)), ((), ())), preferred_element_type=jnp.float32
    )
    logit = raw * scale_ref[0]
    column = lax.broadcasted_iota(jnp.int32, logit.shape, 1) + i * BLK
    hit = lab_ref[...] == column
    kept = jnp.where(jnp.logical_and(valid_ref[...] > 0, jnp.logical_not(hit)), logit, NEG)
    l_scr[:, pl.ds(pl.multiple_of(i * BLK, BLK), BLK)] = kept
    m_scr[...] = jnp.maximum(m_scr[...], jnp.max(kept, axis=1, keepdims=True))
    ll_scr[...] += jnp.sum(jnp.where(hit, logit, 0.0), axis=1, keepdims=True)

    @pl.when(i == pl.num_programs(0) - 1)
    def _():
        rows = l_scr.shape[0]
        half = rows // 2
        step = 32
        lane = lax.broadcasted_iota(jnp.int32, (step, 128), 1)
        tiles = []
        for r in range(0, rows, step):
            top = m_scr[r:r + step, :]
            val = l_scr[r:r + step, :]
            e = jnp.exp(val - top)
            e_ref[r:r + step, :] = e.astype(jnp.bfloat16)
            s = jnp.sum(e, axis=1, keepdims=True)
            t = jnp.sum(e * val, axis=1, keepdims=True)
            tiles.append(
                jnp.where(lane == 0, top, jnp.where(lane == 1, s, jnp.where(lane == 2, t, ll_scr[r:r + step, :])))
            )
        full = jnp.concatenate(tiles, axis=0)
        own = pltpu.roll(full[:half].T, shift_ref[0], 1)
        other = pltpu.roll(full[half:].T, shift_ref[0], 1)
        stat_ref[0:4, :] = own[0:4, :]
        stat_ref[4:8, :] = other[0:4, :]


def logits_call(scale, shift, q, memory, lab, valid):
    rows, depth = q.shape
    n = memory.shape[0]
    return pl.pallas_call(
        logits_kernel,
        grid=(n // BLK,),
        in_specs=[
            pl.BlockSpec(memory_space=pltpu.SMEM),
            pl.BlockSpec(memory_space=pltpu.SMEM),
            pl.BlockSpec((rows, depth), lambda i: (0, 0)),
            pl.BlockSpec((BLK, depth), lambda i: (i, 0)),
            pl.BlockSpec((rows, 1), lambda i: (0, 0)),
            pl.BlockSpec((1, BLK), lambda i: (0, i)),
        ],
        out_specs=[pl.BlockSpec((rows, n), lambda i: (0, 0)), pl.BlockSpec((8, 128), lambda i: (0, 0))],
        out_shape=[
            jax.ShapeDtypeStruct((rows, n), jnp.bfloat16),
            jax.ShapeDtypeStruct((8, 128), jnp.float32),
        ],
        scratch_shapes=[
            pltpu.VMEM((rows, n), jnp.float32),
            pltpu.VMEM((rows, 1), jnp.float32),
            pltpu.VMEM((rows, 1), jnp.float32),
        ],
        compiler_params=pltpu.CompilerParams(vmem_limit_bytes=VMEM),
        cost_estimate=pl.CostEstimate(
            flops=2 * rows * n * depth, bytes_accessed=2 * n * depth, transcendentals=rows * n
        ),
        name="logits",
    )(scale, shift, q, memory, lab, valid)


def product_kernel(e_ref, mem_ref, a_ref, b5_ref, b3_ref):
    out = jnp.dot(e_ref[...], mem_ref[...], preferred_element_type=jnp.float32)
    a_ref[...] = out[0:128].astype(a_ref.dtype)
    b5_ref[...] = out[128:208].astype(b5_ref.dtype)
    b3_ref[...] = out[208:256].astype(b3_ref.dtype)


def product_call(e, memory, own_dtype, name):
    rows, n = e.shape
    depth = memory.shape[1]
    return pl.pallas_call(
        product_kernel,
        grid=(depth // COLS,),
        in_specs=[pl.BlockSpec((rows, n), lambda i: (0, 0)), pl.BlockSpec((n, COLS), lambda i: (0, i))],
        out_specs=[pl.BlockSpec((k, COLS), lambda i: (0, i)) for k in (128, 80, 48)],
        out_shape=[
            jax.ShapeDtypeStruct((128, depth), own_dtype),
            jax.ShapeDtypeStruct((80, depth), jnp.bfloat16),
            jax.ShapeDtypeStruct((48, depth), jnp.bfloat16),
        ],
        compiler_params=pltpu.CompilerParams(vmem_limit_bytes=VMEM),
        cost_estimate=pl.CostEstimate(
            flops=2 * rows * n * depth, bytes_accessed=2 * n * depth, transcendentals=0
        ),
        name=name,
    )(e, memory)


def merge_kernel(z_ref, cot_ref, sets_ref, coef_ref, part_ref):
    z = z_ref[0]
    sets = [sets_ref[lax.rem(a - z + 12, 8)] for a in range(8)]
    top = sets[0][0:1]
    logit = jnp.zeros_like(top)
    for s in sets:
        top = jnp.maximum(top, jnp.maximum(s[0:1], s[4:5]))
        logit = logit + s[3:4] + s[7:8]
    top = jnp.maximum(top, logit)
    rest = jnp.zeros_like(top)
    first = jnp.zeros_like(top)
    for s in sets:
        for k in (0, 4):
            f = jnp.exp(s[k:k + 1] - top)
            rest = rest + f * s[k + 1:k + 2]
            first = first + f * s[k + 2:k + 3]
    total = rest + jnp.exp(logit - top)
    mine = sets_ref[4]
    inverse = 1.0 / total
    label_weight = -rest * inverse
    own = jnp.exp(mine[0:1] - top) * inverse
    other = jnp.exp(mine[4:5] - top) * inverse
    part = cot_ref[...] * (first * inverse + label_weight * logit)
    part_ref[...] = jnp.broadcast_to(jnp.sum(part, axis=1, keepdims=True), part_ref.shape)
    row = lax.broadcasted_iota(jnp.int32, (8, 128), 0)
    stack = jnp.where(row == 0, own, jnp.where(row == 1, other, label_weight))
    back = lax.rem((10 - z) * 16, 128)
    coef_ref[...] = pltpu.roll(stack, back, 1).T


def merge_call(z, cot, sets):
    return pl.pallas_call(
        merge_kernel,
        in_specs=[
            pl.BlockSpec(memory_space=pltpu.SMEM),
            pl.BlockSpec(memory_space=pltpu.VMEM),
            pl.BlockSpec(memory_space=pltpu.VMEM),
        ],
        out_specs=[pl.BlockSpec(memory_space=pltpu.VMEM), pl.BlockSpec(memory_space=pltpu.VMEM)],
        out_shape=[jax.ShapeDtypeStruct((128, 8), jnp.float32), jax.ShapeDtypeStruct((8, 128), jnp.float32)],
        name="merge",
    )(z, cot, sets)


def shards(queries, memory, log_scale, labels, valid, cotangent):
    scale = jnp.exp(log_scale)
    where = lax.axis_index("mem")
    z = lax.rem(where, 8)
    x_lo = where // 8
    start_row = where * memory.shape[0]
    roll_by = lax.rem(z + 6, 8) * 16

    own_labels = lax.dynamic_slice_in_dim(labels, x_lo * 128, 128)
    own_cot = lax.dynamic_slice_in_dim(cotangent, x_lo * 128, 128)
    rolled = lax.dynamic_slice_in_dim(jnp.concatenate([own_labels, own_labels]), roll_by, 128)
    other = send(rolled.astype(jnp.float32), PARTNER).astype(jnp.int32)
    lab = (jnp.concatenate([rolled, other]) - start_row)[:, None]

    up1, down1, up2, down2 = (send(queries, along_z(k)) for k in (1, -1, 2, -2))
    near = jnp.concatenate([up2, up1, queries, down1, down2])
    up3, down3 = send(up2, along_z(1)), send(down2, along_z(-1))
    low4, high4 = send(up2[:8], along_z(2)), send(down2[8:], along_z(-2))
    far = jnp.concatenate([down3, low4, high4, up3])
    near_other = send(near, PARTNER)
    far_other = send(far, PARTNER)
    everything = jnp.concatenate([near, far, near_other, far_other])

    columns = jnp.arange(memory.shape[0], dtype=jnp.int32)
    hits = (lab == columns[None, :]).astype(jnp.bfloat16)
    g_own, g5, g3 = product_call(hits, memory, jnp.bfloat16, "label_rows")
    g5 = send(g5, PARTNER)
    g3 = send(g3, PARTNER)

    shift = roll_by.reshape(1)
    e, stat = logits_call(scale, shift, everything, memory, lab, valid[None, :])
    stat_other = send(stat, PARTNER)
    pair = jnp.concatenate([stat[0:4], stat_other[4:8]])
    o_own, o5, o3 = product_call(e, memory, jnp.float32, "weighted")
    r3 = send(o3, PARTNER)
    r5 = send(o5, PARTNER)
    s_up, s_down = send(pair, along_z(1)), send(pair, along_z(-1))
    three = jnp.stack([s_up, pair, s_down])
    t_up, t_down = send(three, along_z(3)), send(three[:2], along_z(-3))
    sets = jnp.concatenate([t_up, three, t_down])
    coef, part = merge_call(z.reshape(1), own_cot[None, :], sets)

    f32 = jnp.float32
    bf16 = jnp.bfloat16

    def combine(rows, o_other, g_other):
        c = coef[rows]
        g = g_own[rows].astype(f32) + g_other.astype(f32)
        return c[:, 0:1] * o_own[rows] + c[:, 1:2] * o_other.astype(f32) + c[:, 2:3] * g

    p_far = combine(slice(80, 128), r3, g3).astype(bf16)
    p_near = combine(slice(0, 80), r5, g5)
    a3 = send(p_far[0:16], along_z(1))
    a5 = send(p_far[32:48], along_z(-1))
    a4l = send(p_far[16:24], along_z(2))
    a4h = send(p_far[24:32], along_z(-2))
    a1 = send(p_near[48:64].astype(bf16), along_z(1))
    a7 = send(p_near[16:32].astype(bf16), along_z(-1))
    zero = jnp.zeros((8, memory.shape[1]), f32)
    p2 = p_near[64:80] + a3.astype(f32) + jnp.concatenate([a4l.astype(f32), zero])
    p6 = p_near[0:16] + a5.astype(f32) + jnp.concatenate([zero, a4h.astype(f32)])
    a2 = send(p2.astype(bf16), along_z(2))
    a6 = send(p6.astype(bf16), along_z(-2))
    summed = p_near[32:48] + (a1.astype(f32) + a7.astype(f32)) + (a2.astype(f32) + a6.astype(f32))
    q_rows = queries.shape[0]
    my_cot = lax.dynamic_slice_in_dim(cotangent, where * q_rows, q_rows)
    grad_queries = (scale * my_cot[:, None] * summed).astype(bf16)

    for pairs in (CORE, X1, X2, Y1, Y2):
        part = part + send(part, pairs)
    count = cotangent.shape[0] * lax.axis_size("dp")
    scale_grad = part[0, 0:1] / count
    return (grad_queries, scale_grad)


def solution(mesh):
    placed = (P(("dp", "mem"), None), P("mem", None), P(), P("dp"), P("mem"), P("dp"))
    return jax.shard_map(
        shards, mesh=mesh, in_specs=placed, out_specs=(P(("dp", "mem"), None), P()), check_vma=False
    )
```

```python
import functools

import jax
import jax.numpy as jnp
from jax import lax
from jax.experimental import pallas as pl
from jax.experimental.pallas import tpu as pltpu
from jax.sharding import PartitionSpec as P

AXES = ("dp", "mem")
NEG = -1e30
BLK = 512
COLS = 1024


def table(move):
    pairs = []
    for y in range(4):
        for x in range(4):
            for c in range(2):
                for z in range(8):
                    index = lambda y, x, c, z: (((y * 2 + x // 2) * 2 + c) * 2 + x % 2) * 8 + z
                    pairs.append((index(y, x, c, z), index(*move(y, x, c, z))))
    return pairs


def along_z(k):
    return table(lambda y, x, c, z: (y, x, c, (z + k) % 8))


def partner_of(x, c):
    if c == 0:
        return x ^ 1
    return (x + 1) % 4 if x % 2 else (x - 1) % 4


PARTNER = table(lambda y, x, c, z: (y, partner_of(x, c), c, z))
CORE = table(lambda y, x, c, z: (y, x, 1 - c, z))
CROSS = table(lambda y, x, c, z: (y, partner_of(x, 1 - c), c, z))
Y1 = table(lambda y, x, c, z: (y ^ 1, x, c, z))
Y2 = table(lambda y, x, c, z: (y ^ 2, x, c, z))


def send(x, pairs):
    return lax.ppermute(x, AXES, pairs)


def logits_kernel(scale_ref, shift_ref, q_ref, mem_ref, lab_ref, valid_ref, e_ref, stat_ref, l_scr):
    rows, n = l_scr.shape
    scale = scale_ref[0]
    top = jnp.full((rows, 1), NEG, jnp.float32)
    picked = jnp.zeros((rows, 1), jnp.float32)
    for i in range(0, n, BLK):
        raw = lax.dot_general(
            q_ref[...], mem_ref[i:i + BLK, :], (((1,), (1,)), ((), ())), preferred_element_type=jnp.float32
        )
        logit = raw * scale
        column = lax.broadcasted_iota(jnp.int32, logit.shape, 1) + i
        hit = lab_ref[...] == column
        kept = jnp.where(jnp.logical_and(valid_ref[:, i:i + BLK] > 0, jnp.logical_not(hit)), logit, NEG)
        l_scr[:, i:i + BLK] = kept
        top = jnp.maximum(top, jnp.max(kept, axis=1, keepdims=True))
        picked = picked + jnp.sum(jnp.where(hit, logit, 0.0), axis=1, keepdims=True)
    half = rows // 2
    step = 32
    lane = lax.broadcasted_iota(jnp.int32, (step, 128), 1)
    tiles = []
    for r in range(0, rows, step):
        m = top[r:r + step]
        val = l_scr[r:r + step, :]
        e = jnp.exp(val - m)
        e_ref[r:r + step, :] = e.astype(jnp.bfloat16)
        s = jnp.sum(e, axis=1, keepdims=True)
        t = jnp.sum(e * val, axis=1, keepdims=True)
        tiles.append(jnp.where(lane == 0, m, jnp.where(lane == 1, s, jnp.where(lane == 2, t, picked[r:r + step]))))
    full = jnp.concatenate(tiles, axis=0)
    own = pltpu.roll(full[:half].T, shift_ref[0], 1)
    other = pltpu.roll(full[half:].T, shift_ref[0], 1)
    for k in range(4):
        stat_ref[2 * k:2 * k + 1, :] = own[k:k + 1, :]
        stat_ref[2 * k + 1:2 * k + 2, :] = other[k:k + 1, :]


def vmem():
    return pl.BlockSpec(memory_space=pltpu.VMEM)


def smem():
    return pl.BlockSpec(memory_space=pltpu.SMEM)


def params(mib):
    return pltpu.CompilerParams(vmem_limit_bytes=mib * 1024 * 1024)


def logits_call(scale, shift, q, memory, lab, valid):
    rows, depth = q.shape
    n = memory.shape[0]
    return pl.pallas_call(
        logits_kernel,
        in_specs=[smem(), smem(), vmem(), vmem(), vmem(), vmem()],
        out_specs=[vmem(), vmem()],
        out_shape=[
            jax.ShapeDtypeStruct((rows, n), jnp.bfloat16),
            jax.ShapeDtypeStruct((8, 128), jnp.float32),
        ],
        scratch_shapes=[pltpu.VMEM((rows, n), jnp.float32)],
        compiler_params=params(16),
        cost_estimate=pl.CostEstimate(
            flops=2 * rows * n * depth, bytes_accessed=2 * n * depth, transcendentals=rows * n
        ),
        name="logits",
    )(scale, shift, q, memory, lab, valid)


def weighted_kernel(first, e_ref, mem_ref, own_ref, other_ref):
    for c in range(0, own_ref.shape[1], COLS):
        at = slice(c, c + COLS)
        out = jnp.dot(e_ref[...], mem_ref[:, first + c:first + c + COLS], preferred_element_type=jnp.float32)
        own_ref[:, at] = out[:128]
        other_ref[:, at] = out[128:].astype(other_ref.dtype)


def weighted_call(e, memory, first, width):
    rows, n = e.shape
    return pl.pallas_call(
        functools.partial(weighted_kernel, first),
        in_specs=[vmem(), vmem()],
        out_specs=[vmem(), vmem()],
        out_shape=[
            jax.ShapeDtypeStruct((128, width), jnp.float32),
            jax.ShapeDtypeStruct((128, width), jnp.bfloat16),
        ],
        compiler_params=params(16),
        cost_estimate=pl.CostEstimate(flops=2 * rows * n * width, bytes_accessed=2 * n * width, transcendentals=0),
        name="weighted",
    )(e, memory)


def labels_kernel(lab_ref, mem_ref, copy_ref, own_ref, other_ref, hit_scr, sems):
    rows, n = hit_scr.shape
    depth = mem_ref.shape[1]
    pieces = depth // COLS

    def piece(k):
        at = pl.ds(k * COLS, COLS)
        return pltpu.make_async_copy(mem_ref.at[:, at], copy_ref.at[:, at], sems.at[k])

    for k in range(pieces):
        piece(k).start()
    for i in range(0, n, BLK):
        column = lax.broadcasted_iota(jnp.int32, (rows, BLK), 1) + i
        hit_scr[:, i:i + BLK] = jnp.where(lab_ref[...] == column, 1.0, 0.0).astype(jnp.bfloat16)
    for k in range(pieces):
        piece(k).wait()
        c = k * COLS
        out = jnp.dot(hit_scr[...], copy_ref[:, c:c + COLS], preferred_element_type=jnp.float32)
        own_ref[:, c:c + COLS] = out[:128].astype(own_ref.dtype)
        other_ref[:, c:c + COLS] = out[128:].astype(other_ref.dtype)


def labels_call(lab, memory):
    rows = lab.shape[0]
    n, depth = memory.shape
    return pl.pallas_call(
        labels_kernel,
        in_specs=[vmem(), pl.BlockSpec(memory_space=pltpu.HBM)],
        out_specs=[vmem()] * 3,
        out_shape=[
            pltpu.VMEM((n, depth), jnp.bfloat16),
            jax.ShapeDtypeStruct((128, depth), jnp.bfloat16),
            jax.ShapeDtypeStruct((128, depth), jnp.bfloat16),
        ],
        scratch_shapes=[pltpu.VMEM((rows, n), jnp.bfloat16), pltpu.SemaphoreType.DMA((depth // COLS,))],
        compiler_params=params(16),
        cost_estimate=pl.CostEstimate(
            flops=2 * rows * n * depth, bytes_accessed=2 * n * depth, transcendentals=0
        ),
        name="label_rows",
    )(lab, memory)


def mix_kernel(place_ref, cot_ref, up_ref, mid_ref, down_ref, oa_ref, ob_ref, ra_ref, rb_ref, g_ref, gr_ref,
               pu_ref, pd_ref, p4a_ref, p4b_ref, p0_ref, p2_ref, p6_ref, part_ref, sets):
    f32, bf16 = jnp.float32, jnp.bfloat16
    z, x_lo = place_ref[0], place_ref[1]
    sets[0:3] = up_ref[...]
    sets[3:6] = mid_ref[...]
    sets[6:8] = down_ref[...]
    mine, theirs = sets[4, 0], sets[4, 1]
    flat = []
    for a in range(8):
        at = lax.rem(a - z + 12, 8)
        own, other = sets[at, 0], sets[at, 1]
        row = lax.broadcasted_iota(jnp.int32, other.shape, 0)
        swapped = jnp.where(row % 2 == 0, pltpu.roll(other, 7, 0), pltpu.roll(other, 1, 0))
        is_low = x_lo == 0
        flat += [jnp.where(is_low, own, swapped), jnp.where(is_low, swapped, own)]
    top = flat[0][0:2]
    logit = jnp.zeros_like(top)
    for s in flat:
        top = jnp.maximum(top, s[0:2])
        logit = logit + s[6:8]
    top = jnp.maximum(top, logit)
    rest = jnp.zeros_like(top)
    first = jnp.zeros_like(top)
    for s in flat:
        f = jnp.exp(s[0:2] - top)
        rest = rest + f * s[2:4]
        first = first + f * s[4:6]
    inverse = 1.0 / (rest + jnp.exp(logit - top))
    label_weight = -rest * inverse
    part = jnp.sum(cot_ref[...] * (first * inverse + label_weight * logit), axis=1, keepdims=True)
    part_ref[...] = jnp.broadcast_to(part[0:1] + part[1:2], part_ref.shape)
    c_own = jnp.exp(mine[0:1] - top[0:1]) * inverse[0:1]
    c_other = jnp.exp(theirs[1:2] - top[0:1]) * inverse[0:1]
    row = lax.broadcasted_iota(jnp.int32, (8, 128), 0)
    stack = jnp.where(row == 0, c_own, jnp.where(row == 1, c_other, label_weight[0:1]))
    coef = pltpu.roll(stack, lax.rem((10 - z) * 16, 128), 1).T
    half = oa_ref.shape[1]

    def mixed(k):
        at = slice(16 * k, 16 * k + 16)
        c = coef[at]
        sides = []
        for o_ref, r_ref, first in ((oa_ref, ra_ref, 0), (ob_ref, rb_ref, half)):
            cols = slice(first, first + half)
            g = g_ref[at, cols].astype(f32) + gr_ref[at, cols].astype(f32)
            sides.append(c[:, 0:1] * o_ref[at, :] + c[:, 1:2] * r_ref[at, :].astype(f32) + c[:, 2:3] * g)
        return jnp.concatenate(sides, axis=1)

    p6_ref[...] = mixed(0)
    pd_ref[0:16, :] = mixed(1).astype(bf16)
    p0_ref[...] = mixed(2)
    pu_ref[0:16, :] = mixed(3).astype(bf16)
    p2_ref[...] = mixed(4)
    pu_ref[16:32, :] = mixed(5).astype(bf16)
    p4 = mixed(6).astype(bf16)
    p4a_ref[...] = p4[:, :half]
    p4b_ref[...] = p4[:, half:]
    pd_ref[16:32, :] = mixed(7).astype(bf16)


def mix_call(place, cot, up, mid, down, oa, ob, ra, rb, g, gr):
    depth = g.shape[1]
    bf16, f32 = jnp.bfloat16, jnp.float32
    return pl.pallas_call(
        mix_kernel,
        in_specs=[smem()] + [vmem()] * 10,
        out_specs=[vmem()] * 8,
        out_shape=[
            jax.ShapeDtypeStruct((32, depth), bf16),
            jax.ShapeDtypeStruct((32, depth), bf16),
            jax.ShapeDtypeStruct((16, depth // 2), bf16),
            jax.ShapeDtypeStruct((16, depth // 2), bf16),
            jax.ShapeDtypeStruct((16, depth), f32),
            jax.ShapeDtypeStruct((16, depth), f32),
            jax.ShapeDtypeStruct((16, depth), f32),
            jax.ShapeDtypeStruct((8, 128), f32),
        ],
        scratch_shapes=[pltpu.VMEM((8, 2, 8, 128), f32)],
        compiler_params=params(16),
        name="mix",
    )(place, cot, up, mid, down, oa, ob, ra, rb, g, gr)


def shards(queries, memory, log_scale, labels, valid, cotangent):
    f32, bf16 = jnp.float32, jnp.bfloat16
    together = lambda *arrays: lax.optimization_barrier(arrays)
    scale = jnp.exp(log_scale)
    where = lax.axis_index("mem")
    z = lax.rem(where, 8)
    x_lo = where // 8
    half = memory.shape[1] // 2
    start_row = where * memory.shape[0]
    roll_by = lax.rem(z + 6, 8) * 16

    own_labels = lax.dynamic_slice_in_dim(labels, x_lo * 128, 128)
    own_cot = lax.dynamic_slice_in_dim(cotangent, x_lo * 128, 128)
    rolled = lax.dynamic_slice_in_dim(jnp.concatenate([own_labels, own_labels]), roll_by, 128)
    other = send(jnp.stack([rolled.astype(f32), own_cot]), PARTNER)
    lab = (jnp.concatenate([rolled, other[0].astype(jnp.int32)]) - start_row)[:, None]
    cots = jnp.stack([own_cot, other[1]])

    up1, down1, up2, down2 = (send(queries, along_z(k)) for k in (1, -1, 2, -2))
    near = jnp.concatenate([up2, up1, queries, down1, down2])
    up3, down3 = send(up2, along_z(1)), send(down2, along_z(-1))
    low4, high4 = send(up2[:, :half], along_z(2)), send(down2[:, half:], along_z(-2))
    far = jnp.concatenate([down3, jnp.concatenate([low4, high4], axis=1), up3])
    near_other = send(near, PARTNER)
    far_other = send(far, PARTNER)

    late_lab, _ = together(lab, far)
    resident, g, g_other = labels_call(late_lab, pltpu.with_memory_space_constraint(memory, pltpu.HBM))
    resident = pltpu.with_memory_space_constraint(resident, pltpu.VMEM)
    everything = jnp.concatenate([near, far, near_other, far_other])
    g_other = send(g_other, PARTNER)

    e, stat = logits_call(scale, roll_by.reshape(1), everything, resident, lab, valid[None, :])
    stat_other = send(stat, PARTNER)
    e, g_other = together(e, g_other)
    oa, o_other = weighted_call(e, resident, 0, half)
    stat_other, o_other, e = together(stat_other, o_other, e)
    ra = send(o_other, PARTNER)
    pair = jnp.stack([stat, stat_other])
    ob, o_other = weighted_call(e, resident, half, half)
    rb = send(o_other, PARTNER)
    s_up, s_down = send(pair, along_z(1)), send(pair, along_z(-1))
    three = jnp.stack([s_up, pair, s_down])
    t_up, t_down = send(three, along_z(3)), send(three[:2], along_z(-3))
    pu, pd, p4a, p4b, p0, p2, p6, part = mix_call(
        jnp.stack([z, x_lo]), cots, t_up, three, t_down, oa, ob, ra, rb, g, g_other
    )
    au, ad = send(pu, along_z(1)), send(pd, along_z(-1))
    a4a, a4b = send(p4a, along_z(2)), send(p4b, along_z(-2))
    part = part + send(part, CROSS)
    au, ad, a4a, a4b, part = together(au, ad, a4a, a4b, part)
    zero = jnp.zeros((16, half), f32)
    p2 = p2 + au[16:].astype(f32) + jnp.concatenate([a4a.astype(f32), zero], axis=1)
    p6 = p6 + ad[16:].astype(f32) + jnp.concatenate([zero, a4b.astype(f32)], axis=1)
    a2 = send(p2.astype(bf16), along_z(2))
    a6 = send(p6.astype(bf16), along_z(-2))
    for pairs in (CORE, Y1, Y2):
        part = part + send(part, pairs)
    summed = p0 + (au[:16].astype(f32) + ad[:16].astype(f32)) + (a2.astype(f32) + a6.astype(f32))
    q_rows = queries.shape[0]
    my_cot = lax.dynamic_slice_in_dim(cotangent, where * q_rows, q_rows)
    grad_queries = (scale * my_cot[:, None] * summed).astype(bf16)

    count = cotangent.shape[0] * lax.axis_size("dp")
    scale_grad = part[0, 0:1] / count
    return (grad_queries, scale_grad)


def solution(mesh):
    placed = (P(("dp", "mem"), None), P("mem", None), P(), P("dp"), P("mem"), P("dp"))
    return jax.shard_map(
        shards, mesh=mesh, in_specs=placed, out_specs=(P(("dp", "mem"), None), P()), check_vma=False
    )
```

```python
import jax
import jax.numpy as jnp
from jax import lax
from jax.experimental import pallas as pl
from jax.experimental.pallas import tpu as pltpu
from jax.sharding import PartitionSpec as P

AXES = ("dp", "mem")
NEG = -1e30
BLK = 512
COLS = 1024


def table(move):
    pairs = []
    for y in range(4):
        for x in range(4):
            for c in range(2):
                for z in range(8):
                    index = lambda y, x, c, z: (((y * 2 + x // 2) * 2 + c) * 2 + x % 2) * 8 + z
                    pairs.append((index(y, x, c, z), index(*move(y, x, c, z))))
    return pairs


def along_z(k):
    return table(lambda y, x, c, z: (y, x, c, (z + k) % 8))


def partner_of(x, c):
    if c == 0:
        return x ^ 1
    return (x + 1) % 4 if x % 2 else (x - 1) % 4


PARTNER = table(lambda y, x, c, z: (y, partner_of(x, c), c, z))
CORE = table(lambda y, x, c, z: (y, x, 1 - c, z))
CROSS = table(lambda y, x, c, z: (y, partner_of(x, 1 - c), c, z))
Y1 = table(lambda y, x, c, z: (y ^ 1, x, c, z))
Y2 = table(lambda y, x, c, z: (y ^ 2, x, c, z))


def send(x, pairs):
    return lax.ppermute(x, AXES, pairs)


def both(up, down, k):
    down = send(down, along_z(-k))
    return send(up, along_z(k)), down


def fill(q_scr, first, own, two, up, down):
    depth = q_scr.shape[1]
    half = depth // 2
    near, next_, last = slice(0, depth), slice(depth, 2 * depth), slice(2 * depth, 2 * depth + half)
    places = (down, next_), (up, near), (own, near), (down, near), (up, next_), (two, next_), None, (two, near)
    for k, place in enumerate(places):
        if place is not None:
            q_scr[first + 16 * k:first + 16 * k + 16, :] = place[0][:, place[1]]
    q_scr[first + 96:first + 112, :half] = up[:, last]
    q_scr[first + 96:first + 112, half:] = down[:, last]


def pack_kernel(own_ref, up3_ref, down3_ref, lab_ref, cot_ref, up_ref, down_ref, two_ref, sems):
    f32, bf16 = jnp.float32, jnp.bfloat16
    depth = up3_ref.shape[1]
    half = depth // 2
    copies = [
        pltpu.make_async_copy(own_ref, ref.at[:, pl.ds(0, depth)], sems.at[k]) for k, ref in enumerate((up_ref, down_ref))
    ]
    for copy in copies:
        copy.start()
    up_ref[:, depth:2 * depth] = down3_ref[...]
    up_ref[:, 2 * depth:] = up3_ref[:, :half]
    down_ref[:, depth:2 * depth] = up3_ref[...]
    down_ref[:, 2 * depth:] = down3_ref[:, half:]
    two_ref[:, :depth] = up3_ref[...]
    two_ref[:, depth:2 * depth] = down3_ref[...]
    label = lab_ref[...]
    high = lax.shift_right_logical(label, 8)
    rest = cot_ref[...]
    terms = [high.astype(f32), (label - high * 256).astype(f32)]
    for _ in range(3):
        term = rest.astype(bf16).astype(f32)
        terms.append(term)
        rest = rest - term
    row = lax.broadcasted_iota(jnp.int32, (16, 128), 0)
    note = jnp.zeros((16, 128), f32)
    for k, term in enumerate(terms):
        note = jnp.where(row == k, term, note)
    two_ref[:, 2 * depth:] = note.astype(bf16)
    for copy in copies:
        copy.wait()


def pack_call(own, up3, down3, lab, cot):
    rows, depth = own.shape
    wide = 2 * depth + depth // 2
    return pl.pallas_call(
        pack_kernel,
        in_specs=[hbm()] + [vmem()] * 4,
        out_specs=[vmem()] * 3,
        out_shape=[jax.ShapeDtypeStruct((rows, k), jnp.bfloat16) for k in (wide, wide, 2 * depth + 128)],
        scratch_shapes=[pltpu.SemaphoreType.DMA((2,))],
        compiler_params=params(4),
        name="pack",
    )(pltpu.with_memory_space_constraint(own, pltpu.HBM), up3, down3, lab, cot)


def logits_kernel(scale_ref, shift_ref, own, two, up, down, own_x, two_x, up_x, down_x,
                  mem_ref, lab_ref, valid_ref, e_ref, stat_ref, q_scr, l_scr):
    fill(q_scr, 0, own, two, up, down)
    fill(q_scr, 128, own_x, two_x, up_x, down_x)
    rows, n = l_scr.shape
    scale = scale_ref[0]
    top = jnp.full((rows, 1), NEG, jnp.float32)
    picked = jnp.zeros((rows, 1), jnp.float32)
    for i in range(0, n, BLK):
        raw = lax.dot_general(
            q_scr[...], mem_ref[i:i + BLK, :], (((1,), (1,)), ((), ())), preferred_element_type=jnp.float32
        )
        logit = raw * scale
        column = lax.broadcasted_iota(jnp.int32, logit.shape, 1) + i
        hit = lab_ref[...] == column
        kept = jnp.where(jnp.logical_and(valid_ref[:, i:i + BLK] > 0, jnp.logical_not(hit)), logit, NEG)
        l_scr[:, i:i + BLK] = kept
        top = jnp.maximum(top, jnp.max(kept, axis=1, keepdims=True))
        picked = picked + jnp.sum(jnp.where(hit, logit, 0.0), axis=1, keepdims=True)
    half = rows // 2
    step = 32
    lane = lax.broadcasted_iota(jnp.int32, (step, 128), 1)
    tiles = []
    for r in range(0, rows, step):
        m = top[r:r + step]
        val = l_scr[r:r + step, :]
        e = jnp.exp(val - m)
        e_ref[r:r + step, :] = e.astype(jnp.bfloat16)
        s = jnp.sum(e, axis=1, keepdims=True)
        t = jnp.sum(e * val, axis=1, keepdims=True)
        tiles.append(jnp.where(lane == 0, m, jnp.where(lane == 1, s, jnp.where(lane == 2, t, picked[r:r + step]))))
    full = jnp.concatenate(tiles, axis=0)
    own = pltpu.roll(full[:half].T, shift_ref[0], 1)
    other = pltpu.roll(full[half:].T, shift_ref[0], 1)
    for k in range(4):
        stat_ref[2 * k:2 * k + 1, :] = own[k:k + 1, :]
        stat_ref[2 * k + 1:2 * k + 2, :] = other[k:k + 1, :]


def vmem():
    return pl.BlockSpec(memory_space=pltpu.VMEM)


def smem():
    return pl.BlockSpec(memory_space=pltpu.SMEM)


def params(mib):
    return pltpu.CompilerParams(vmem_limit_bytes=mib * 1024 * 1024)


def logits_call(scale, shift, blocks, memory, lab, valid):
    n, depth = memory.shape
    rows = lab.shape[0]
    return pl.pallas_call(
        logits_kernel,
        in_specs=[smem(), smem()] + [vmem()] * (len(blocks) + 3),
        out_specs=[vmem(), vmem()],
        out_shape=[
            jax.ShapeDtypeStruct((rows, n), jnp.bfloat16),
            jax.ShapeDtypeStruct((8, 128), jnp.float32),
        ],
        scratch_shapes=[
            pltpu.VMEM((rows, depth), jnp.bfloat16),
            pltpu.VMEM((rows, n), jnp.float32),
        ],
        compiler_params=params(8),
        cost_estimate=pl.CostEstimate(
            flops=2 * rows * n * depth, bytes_accessed=2 * n * depth, transcendentals=rows * n
        ),
        name="logits",
    )(scale, shift, *blocks, memory, lab, valid)


FIRST = (3, 0, 6, 1, 4)
SECOND = (2, 5, 7)


def weighted_kernel(e_ref, mem_ref, g_ref, own_ref, first_ref, second_ref):
    second_ref[16 * len(SECOND):, :] = g_ref[...]
    for c in range(0, mem_ref.shape[1], COLS):
        at = slice(c, c + COLS)
        out = jnp.dot(e_ref[...], mem_ref[:, at], preferred_element_type=jnp.float32)
        spread(out, at, own_ref, first_ref, second_ref)


def spread(out, at, own_ref, first_ref, second_ref):
    own_ref[:, at] = out[:128].astype(own_ref.dtype)
    for ref, order in ((first_ref, FIRST), (second_ref, SECOND)):
        for i, k in enumerate(order):
            ref[16 * i:16 * i + 16, at] = out[128 + 16 * k:144 + 16 * k].astype(ref.dtype)


def weighted_call(e, memory, g):
    rows, n = e.shape
    depth = memory.shape[1]
    return pl.pallas_call(
        weighted_kernel,
        in_specs=[vmem()] * 3,
        out_specs=[vmem()] * 3,
        out_shape=[
            jax.ShapeDtypeStruct((128, depth), jnp.float32),
            jax.ShapeDtypeStruct((16 * len(FIRST), depth), jnp.bfloat16),
            jax.ShapeDtypeStruct((32 * len(SECOND), depth), jnp.bfloat16),
        ],
        compiler_params=params(8),
        cost_estimate=pl.CostEstimate(flops=2 * rows * n * depth, bytes_accessed=2 * n * depth, transcendentals=0),
        name="weighted",
    )(e, memory, g)


def labels_kernel(lab_ref, mem_ref, copy_ref, own_ref, first_ref, second_ref, hit_scr, sems):
    rows, n = hit_scr.shape
    pieces = mem_ref.shape[1] // COLS

    def piece(k):
        at = pl.ds(k * COLS, COLS)
        return pltpu.make_async_copy(mem_ref.at[:, at], copy_ref.at[:, at], sems.at[k])

    for k in range(pieces):
        piece(k).start()
    for i in range(0, n, BLK):
        column = lax.broadcasted_iota(jnp.int32, (rows, BLK), 1) + i
        hit_scr[:, i:i + BLK] = jnp.where(lab_ref[...] == column, 1.0, 0.0).astype(jnp.bfloat16)
    for k in range(pieces):
        piece(k).wait()
        at = slice(k * COLS, k * COLS + COLS)
        out = jnp.dot(hit_scr[...], copy_ref[:, at], preferred_element_type=jnp.float32)
        spread(out, at, own_ref, first_ref, second_ref)


def hbm():
    return pl.BlockSpec(memory_space=pltpu.HBM)


def labels_call(lab, memory):
    rows = lab.shape[0]
    n, depth = memory.shape
    return pl.pallas_call(
        labels_kernel,
        in_specs=[vmem(), hbm()],
        out_specs=[vmem()] * 4,
        out_shape=[
            pltpu.VMEM((n, depth), jnp.bfloat16),
            jax.ShapeDtypeStruct((128, depth), jnp.bfloat16),
            jax.ShapeDtypeStruct((16 * len(FIRST), depth), jnp.bfloat16),
            jax.ShapeDtypeStruct((16 * len(SECOND), depth), jnp.bfloat16),
        ],
        scratch_shapes=[pltpu.VMEM((rows, n), jnp.bfloat16), pltpu.SemaphoreType.DMA((depth // COLS,))],
        compiler_params=params(8),
        cost_estimate=pl.CostEstimate(
            flops=2 * rows * n * depth, bytes_accessed=2 * n * depth, transcendentals=0
        ),
        name="label_rows",
    )(lab, pltpu.with_memory_space_constraint(memory, pltpu.HBM))


def merge_kernel(place_ref, cot_ref, up_ref, mid_ref, down_ref, coef_ref, part_ref, sets):
    z, x_lo = place_ref[0], place_ref[1]
    sets[0:3] = up_ref[...]
    sets[3:6] = mid_ref[...]
    sets[6:8] = down_ref[...]
    mine, theirs = sets[4, 0], sets[4, 1]
    flat = []
    for a in range(8):
        at = lax.rem(a - z + 12, 8)
        own, other = sets[at, 0], sets[at, 1]
        row = lax.broadcasted_iota(jnp.int32, other.shape, 0)
        swapped = jnp.where(row % 2 == 0, pltpu.roll(other, 7, 0), pltpu.roll(other, 1, 0))
        is_low = x_lo == 0
        flat += [jnp.where(is_low, own, swapped), jnp.where(is_low, swapped, own)]
    top = flat[0][0:2]
    logit = jnp.zeros_like(top)
    for s in flat:
        top = jnp.maximum(top, s[0:2])
        logit = logit + s[6:8]
    top = jnp.maximum(top, logit)
    rest = jnp.zeros_like(top)
    first = jnp.zeros_like(top)
    for s in flat:
        f = jnp.exp(s[0:2] - top)
        rest = rest + f * s[2:4]
        first = first + f * s[4:6]
    inverse = 1.0 / (rest + jnp.exp(logit - top))
    label_weight = -rest * inverse
    part = jnp.sum(cot_ref[...] * (first * inverse + label_weight * logit), axis=1, keepdims=True)
    part_ref[...] = jnp.broadcast_to(part[0:1] + part[1:2], part_ref.shape)
    c_own = jnp.exp(mine[0:1] - top[0:1]) * inverse[0:1]
    c_other = jnp.exp(theirs[1:2] - top[0:1]) * inverse[0:1]
    row = lax.broadcasted_iota(jnp.int32, (8, 128), 0)
    stack = jnp.where(row == 0, c_own, jnp.where(row == 1, c_other, label_weight[0:1]))
    coef_ref[...] = pltpu.roll(stack, lax.rem((10 - z) * 16, 128), 1).T


def merge_call(place, cot, up, mid, down):
    return pl.pallas_call(
        merge_kernel,
        in_specs=[smem()] + [vmem()] * 4,
        out_specs=[vmem()] * 2,
        out_shape=[jax.ShapeDtypeStruct((128, 8), jnp.float32), jax.ShapeDtypeStruct((8, 128), jnp.float32)],
        scratch_shapes=[pltpu.VMEM((8, 2, 8, 128), jnp.float32)],
        compiler_params=params(4),
        name="merge",
    )(place, cot, up, mid, down)


def mix_kernel(coef_ref, o_ref, r_ref, g_ref, gr_ref, pu_ref, pd_ref):
    bf16 = jnp.bfloat16
    half = o_ref.shape[1] // 2
    depth = 2 * half
    for i, (ref, first) in enumerate(((pu_ref, 0), (pu_ref, depth), (None, 0), (pd_ref, 0), (pd_ref, depth))):
        p = mixed(coef_ref, o_ref, r_ref, g_ref, gr_ref, FIRST[i], i, i).astype(bf16)
        if i == 2:
            pu_ref[:, 2 * depth:] = p[:, :half]
            pd_ref[:, 2 * depth:] = p[:, half:]
        else:
            ref[:, first:first + depth] = p


def mixed(coef_ref, o_ref, r_ref, g_ref, gr_ref, k, i, j):
    f32 = jnp.float32
    at, there = slice(16 * k, 16 * k + 16), slice(16 * i, 16 * i + 16)
    label = slice(16 * j, 16 * j + 16)
    c = coef_ref[at, :]
    g = g_ref[at, :].astype(f32) + gr_ref[label, :].astype(f32)
    return c[:, 0:1] * o_ref[at, :] + c[:, 1:2] * r_ref[there, :].astype(f32) + c[:, 2:3] * g


def mix_call(coef, o, r, g, gr):
    depth = g.shape[1]
    bf16 = jnp.bfloat16
    return pl.pallas_call(
        mix_kernel,
        in_specs=[vmem()] * 5,
        out_specs=[vmem()] * 2,
        out_shape=[jax.ShapeDtypeStruct((16, 2 * depth + depth // 2), bf16)] * 2,
        compiler_params=params(8),
        name="mix",
    )(coef, o, r, g, gr)


def rest_kernel(coef_ref, o_ref, r_ref, g_ref, *outs):
    for i, out in enumerate(outs):
        out[...] = mixed(coef_ref, o_ref, r_ref, g_ref, r_ref, SECOND[i], i, i + len(SECOND))


def rest_call(coef, o, r, g):
    depth = g.shape[1]
    return pl.pallas_call(
        rest_kernel,
        in_specs=[vmem()] * 4,
        out_specs=[vmem()] * 3,
        out_shape=[jax.ShapeDtypeStruct((16, depth), jnp.float32)] * 3,
        compiler_params=params(8),
        name="rest",
    )(coef, o, r, g)


def shards(queries, memory, log_scale, labels, valid, cotangent):
    f32, bf16 = jnp.float32, jnp.bfloat16
    together = lambda *arrays: lax.optimization_barrier(arrays)
    scale = jnp.exp(log_scale)
    where = lax.axis_index("mem")
    z = lax.rem(where, 8)
    x_lo = where // 8
    depth = memory.shape[1]
    half = depth // 2
    start_row = where * memory.shape[0]
    roll_by = lax.rem(z + 6, 8) * 16

    up3, down3 = both(queries, queries, 3)
    own_labels = lax.dynamic_slice_in_dim(labels, x_lo * 128, 128)
    own_cot = lax.dynamic_slice_in_dim(cotangent, x_lo * 128, 128)
    rolled = lax.dynamic_slice_in_dim(jnp.concatenate([own_labels, own_labels]), roll_by, 128)
    up3, late_queries = together(up3, queries)
    to_up, to_down, to_x = pack_call(late_queries, up3, down3, rolled[None, :], own_cot[None, :])
    up, down = both(to_up, to_down, 1)
    own_x = send(queries, PARTNER)
    two_x = send(to_x, PARTNER)
    note = two_x[:, 2 * depth:].astype(f32)
    lab = (jnp.concatenate([rolled, (note[0] * 256.0 + note[1]).astype(jnp.int32)]) - start_row)[:, None]
    cots = jnp.stack([own_cot, (note[2] + note[3]) + note[4]])
    up, down, lab = together(up, down, lab)
    up_x, down_x = send(up, PARTNER), send(down, PARTNER)
    resident, g, g_first, g_second = labels_call(lab, memory)
    resident = pltpu.with_memory_space_constraint(resident, pltpu.VMEM)
    g_first_x = send(g_first, PARTNER)
    blocks = (to_up, to_x, up, down, own_x, two_x, up_x, down_x)

    e, stat = logits_call(scale, roll_by.reshape(1), blocks, resident, lab, valid[None, :])
    stat_other = send(stat, PARTNER)
    o, o_first, o_second = weighted_call(e, resident, g_second)
    stat_other, o_first, o_second, g_first_x = together(stat_other, o_first, o_second, g_first_x)
    r_first = send(o_first, PARTNER)
    pair = jnp.stack([stat, stat_other])
    s_up, s_down = both(pair, pair, 1)
    s_up, s_down, o_second = together(s_up, s_down, o_second)
    r_second = send(o_second, PARTNER)
    three = jnp.stack([s_up, pair, s_down])
    t_up, t_down = both(three, three[:2], 3)
    t_up, late_z, late_x = together(t_up, z, x_lo)
    coef, part = merge_call(jnp.stack([late_z, late_x]), cots, t_up, three, t_down)
    pu, pd = mix_call(coef, o, r_first, g, g_first_x)
    au, ad = both(pu, pd, 1)
    p0, p3, p5 = rest_call(coef, o, r_second, g)
    for pairs in (CROSS, CORE):
        part = part + send(part, pairs)
    au, ad, part, p0, p3, p5 = together(au, ad, part, p0, p3, p5)
    zero = jnp.zeros((16, half), f32)
    near, next_, last = slice(0, depth), slice(depth, 2 * depth), slice(2 * depth, 2 * depth + half)
    p3 = p3 + ad[:, next_].astype(f32) + jnp.concatenate([au[:, last].astype(f32), zero], axis=1)
    p5 = p5 + au[:, next_].astype(f32) + jnp.concatenate([zero, ad[:, last].astype(f32)], axis=1)
    p3, p5, part = together(p3.astype(bf16), p5.astype(bf16), part)
    a3, a5 = both(p3, p5, 3)
    for pairs in (Y1, Y2):
        part = part + send(part, pairs)
    summed = p0 + (au[:, near].astype(f32) + ad[:, near].astype(f32)) + (a3.astype(f32) + a5.astype(f32))
    q_rows = queries.shape[0]
    a3, last_cot = together(a3, cotangent)
    my_cot = lax.dynamic_slice_in_dim(last_cot, where * q_rows, q_rows)
    grad_queries = (scale * my_cot[:, None] * summed).astype(bf16)

    count = cotangent.shape[0] * lax.axis_size("dp")
    scale_grad = part[0, 0:1] / count
    return (grad_queries, scale_grad)


def solution(mesh):
    placed = (P(("dp", "mem"), None), P("mem", None), P(), P("dp"), P("mem"), P("dp"))
    return jax.shard_map(
        shards, mesh=mesh, in_specs=placed, out_specs=(P(("dp", "mem"), None), P()), check_vma=False
    )
```

```python
import jax
import jax.numpy as jnp
from jax import lax
from jax.experimental import pallas as pl
from jax.experimental.pallas import tpu as pltpu
from jax.sharding import PartitionSpec as P

AXES = ("dp", "mem")
NEG = -1e30
BLK = 512
COLS = 1024


def table(move):
    pairs = []
    for y in range(4):
        for x in range(4):
            for c in range(2):
                for z in range(8):
                    index = lambda y, x, c, z: (((y * 2 + x // 2) * 2 + c) * 2 + x % 2) * 8 + z
                    pairs.append((index(y, x, c, z), index(*move(y, x, c, z))))
    return pairs


def along_z(k):
    return table(lambda y, x, c, z: (y, x, c, (z + k) % 8))


def partner_of(x, c):
    if c == 0:
        return x ^ 1
    return (x + 1) % 4 if x % 2 else (x - 1) % 4


PARTNER = table(lambda y, x, c, z: (y, partner_of(x, c), c, z))
CORE = table(lambda y, x, c, z: (y, x, 1 - c, z))
CROSS = table(lambda y, x, c, z: (y, partner_of(x, 1 - c), c, z))
Y1 = table(lambda y, x, c, z: (y ^ 1, x, c, z))
Y2 = table(lambda y, x, c, z: (y ^ 2, x, c, z))


def send(x, pairs):
    return lax.ppermute(x, AXES, pairs)


def both(up, down, k):
    down = send(down, along_z(-k))
    return send(up, along_z(k)), down


def fill(q_scr, first, three, up, down):
    depth = q_scr.shape[1]
    half = depth // 2
    near, next_, last = slice(0, depth), slice(depth, 2 * depth), slice(2 * depth, 2 * depth + half)
    third = slice(2 * depth, 3 * depth)
    places = (down, next_), (up, near), (three, near), (down, near), (up, next_), (three, third), None, (three, next_)
    for k, place in enumerate(places):
        if place is not None:
            q_scr[first + 16 * k:first + 16 * k + 16, :] = place[0][:, place[1]]
    q_scr[first + 96:first + 112, :half] = up[:, last]
    q_scr[first + 96:first + 112, half:] = down[:, last]


def pack_kernel(own_ref, up3_ref, down3_ref, lab_ref, cot_ref, up_ref, down_ref, three_ref, sems):
    f32, bf16 = jnp.float32, jnp.bfloat16
    depth = up3_ref.shape[1]
    half = depth // 2
    copies = [
        pltpu.make_async_copy(own_ref, ref.at[:, pl.ds(0, depth)], sems.at[k]) for k, ref in enumerate((up_ref, down_ref, three_ref))
    ]
    for copy in copies:
        copy.start()
    up_ref[:, depth:2 * depth] = down3_ref[...]
    up_ref[:, 2 * depth:] = up3_ref[:, :half]
    down_ref[:, depth:2 * depth] = up3_ref[...]
    down_ref[:, 2 * depth:] = down3_ref[:, half:]
    three_ref[:, depth:2 * depth] = up3_ref[...]
    three_ref[:, 2 * depth:3 * depth] = down3_ref[...]
    label = lab_ref[...]
    high = lax.shift_right_logical(label, 8)
    rest = cot_ref[...]
    terms = [high.astype(f32), (label - high * 256).astype(f32)]
    for _ in range(3):
        term = rest.astype(bf16).astype(f32)
        terms.append(term)
        rest = rest - term
    row = lax.broadcasted_iota(jnp.int32, (16, 128), 0)
    note = jnp.zeros((16, 128), f32)
    for k, term in enumerate(terms):
        note = jnp.where(row == k, term, note)
    three_ref[:, 3 * depth:] = note.astype(bf16)
    for copy in copies:
        copy.wait()


def pack_call(own, up3, down3, lab, cot):
    rows, depth = own.shape
    wide = 2 * depth + depth // 2
    return pl.pallas_call(
        pack_kernel,
        in_specs=[hbm()] + [vmem()] * 4,
        out_specs=[vmem()] * 3,
        out_shape=[jax.ShapeDtypeStruct((rows, k), jnp.bfloat16) for k in (wide, wide, 3 * depth + 128)],
        scratch_shapes=[pltpu.SemaphoreType.DMA((3,))],
        compiler_params=params(4),
        name="pack",
    )(pltpu.with_memory_space_constraint(own, pltpu.HBM), up3, down3, lab, cot)


def logits_kernel(scale_ref, shift_ref, three, up, down, three_x, up_x, down_x,
                  mem_ref, lab_ref, valid_ref, e_ref, stat_ref, q_scr, l_scr):
    fill(q_scr, 0, three, up, down)
    fill(q_scr, 128, three_x, up_x, down_x)
    rows, n = l_scr.shape
    scale = scale_ref[0]
    top = jnp.full((rows, 1), NEG, jnp.float32)
    picked = jnp.zeros((rows, 1), jnp.float32)
    for i in range(0, n, BLK):
        raw = lax.dot_general(
            q_scr[...], mem_ref[i:i + BLK, :], (((1,), (1,)), ((), ())), preferred_element_type=jnp.float32
        )
        logit = raw * scale
        column = lax.broadcasted_iota(jnp.int32, logit.shape, 1) + i
        hit = lab_ref[...] == column
        kept = jnp.where(jnp.logical_and(valid_ref[:, i:i + BLK] > 0, jnp.logical_not(hit)), logit, NEG)
        l_scr[:, i:i + BLK] = kept
        top = jnp.maximum(top, jnp.max(kept, axis=1, keepdims=True))
        picked = picked + jnp.sum(jnp.where(hit, logit, 0.0), axis=1, keepdims=True)
    half = rows // 2
    step = 32
    lane = lax.broadcasted_iota(jnp.int32, (step, 128), 1)
    tiles = []
    for r in range(0, rows, step):
        m = top[r:r + step]
        val = l_scr[r:r + step, :]
        e = jnp.exp(val - m)
        e_ref[r:r + step, :] = e.astype(jnp.bfloat16)
        s = jnp.sum(e, axis=1, keepdims=True)
        t = jnp.sum(e * val, axis=1, keepdims=True)
        tiles.append(jnp.where(lane == 0, m, jnp.where(lane == 1, s, jnp.where(lane == 2, t, picked[r:r + step]))))
    full = jnp.concatenate(tiles, axis=0)
    own = pltpu.roll(full[:half].T, shift_ref[0], 1)
    other = pltpu.roll(full[half:].T, shift_ref[0], 1)
    for k in range(4):
        stat_ref[2 * k:2 * k + 1, :] = own[k:k + 1, :]
        stat_ref[2 * k + 1:2 * k + 2, :] = other[k:k + 1, :]


def vmem():
    return pl.BlockSpec(memory_space=pltpu.VMEM)


def smem():
    return pl.BlockSpec(memory_space=pltpu.SMEM)


def params(mib):
    return pltpu.CompilerParams(vmem_limit_bytes=mib * 1024 * 1024)


def logits_call(scale, shift, blocks, memory, lab, valid):
    n, depth = memory.shape
    rows = lab.shape[0]
    return pl.pallas_call(
        logits_kernel,
        in_specs=[smem(), smem()] + [vmem()] * (len(blocks) + 3),
        out_specs=[vmem(), vmem()],
        out_shape=[
            jax.ShapeDtypeStruct((rows, n), jnp.bfloat16),
            jax.ShapeDtypeStruct((8, 128), jnp.float32),
        ],
        scratch_shapes=[
            pltpu.VMEM((rows, depth), jnp.bfloat16),
            pltpu.VMEM((rows, n), jnp.float32),
        ],
        compiler_params=params(8),
        cost_estimate=pl.CostEstimate(
            flops=2 * rows * n * depth, bytes_accessed=2 * n * depth, transcendentals=rows * n
        ),
        name="logits",
    )(scale, shift, *blocks, memory, lab, valid)


FIRST = (3, 0, 6, 1, 4)
SECOND = (2, 5, 7)


def weighted_kernel(e_ref, mem_ref, g_ref, own_ref, first_ref, second_ref):
    second_ref[16 * len(SECOND):, :] = g_ref[...]
    for c in range(0, mem_ref.shape[1], COLS):
        at = slice(c, c + COLS)
        out = jnp.dot(e_ref[...], mem_ref[:, at], preferred_element_type=jnp.float32)
        spread(out, at, own_ref, first_ref, second_ref)


def spread(out, at, own_ref, first_ref, second_ref):
    own_ref[:, at] = out[:128].astype(own_ref.dtype)
    for ref, order in ((first_ref, FIRST), (second_ref, SECOND)):
        for i, k in enumerate(order):
            ref[16 * i:16 * i + 16, at] = out[128 + 16 * k:144 + 16 * k].astype(ref.dtype)


def weighted_call(e, memory, g):
    rows, n = e.shape
    depth = memory.shape[1]
    return pl.pallas_call(
        weighted_kernel,
        in_specs=[vmem()] * 3,
        out_specs=[vmem()] * 3,
        out_shape=[
            jax.ShapeDtypeStruct((128, depth), jnp.float32),
            jax.ShapeDtypeStruct((16 * len(FIRST), depth), jnp.bfloat16),
            jax.ShapeDtypeStruct((32 * len(SECOND), depth), jnp.bfloat16),
        ],
        compiler_params=params(8),
        cost_estimate=pl.CostEstimate(flops=2 * rows * n * depth, bytes_accessed=2 * n * depth, transcendentals=0),
        name="weighted",
    )(e, memory, g)


def labels_kernel(lab_ref, mem_ref, copy_ref, own_ref, first_ref, second_ref, hit_scr, sems):
    rows, n = hit_scr.shape
    pieces = mem_ref.shape[1] // COLS

    def piece(k):
        at = pl.ds(k * COLS, COLS)
        return pltpu.make_async_copy(mem_ref.at[:, at], copy_ref.at[:, at], sems.at[k])

    for k in range(pieces):
        piece(k).start()
    for i in range(0, n, BLK):
        column = lax.broadcasted_iota(jnp.int32, (rows, BLK), 1) + i
        hit_scr[:, i:i + BLK] = jnp.where(lab_ref[...] == column, 1.0, 0.0).astype(jnp.bfloat16)
    for k in range(pieces):
        piece(k).wait()
        at = slice(k * COLS, k * COLS + COLS)
        out = jnp.dot(hit_scr[...], copy_ref[:, at], preferred_element_type=jnp.float32)
        spread(out, at, own_ref, first_ref, second_ref)


def hbm():
    return pl.BlockSpec(memory_space=pltpu.HBM)


def labels_call(lab, memory):
    rows = lab.shape[0]
    n, depth = memory.shape
    return pl.pallas_call(
        labels_kernel,
        in_specs=[vmem(), hbm()],
        out_specs=[vmem()] * 4,
        out_shape=[
            pltpu.VMEM((n, depth), jnp.bfloat16),
            jax.ShapeDtypeStruct((128, depth), jnp.bfloat16),
            jax.ShapeDtypeStruct((16 * len(FIRST), depth), jnp.bfloat16),
            jax.ShapeDtypeStruct((16 * len(SECOND), depth), jnp.bfloat16),
        ],
        scratch_shapes=[pltpu.VMEM((rows, n), jnp.bfloat16), pltpu.SemaphoreType.DMA((depth // COLS,))],
        compiler_params=params(8),
        cost_estimate=pl.CostEstimate(flops=1024, bytes_accessed=1024, transcendentals=0),
        name="label_rows",
    )(lab, pltpu.with_memory_space_constraint(memory, pltpu.HBM))


def merge_kernel(place_ref, cot_ref, up_ref, mid_ref, down_ref, coef_ref, part_ref, sets):
    z, x_lo = place_ref[0], place_ref[1]
    sets[0:3] = up_ref[...]
    sets[3:6] = mid_ref[...]
    sets[6:8] = down_ref[...]
    mine, theirs = sets[4, 0], sets[4, 1]
    flat = []
    for a in range(8):
        at = lax.rem(a - z + 12, 8)
        own, other = sets[at, 0], sets[at, 1]
        row = lax.broadcasted_iota(jnp.int32, other.shape, 0)
        swapped = jnp.where(row % 2 == 0, pltpu.roll(other, 7, 0), pltpu.roll(other, 1, 0))
        is_low = x_lo == 0
        flat += [jnp.where(is_low, own, swapped), jnp.where(is_low, swapped, own)]
    top = flat[0][0:2]
    logit = jnp.zeros_like(top)
    for s in flat:
        top = jnp.maximum(top, s[0:2])
        logit = logit + s[6:8]
    top = jnp.maximum(top, logit)
    rest = jnp.zeros_like(top)
    first = jnp.zeros_like(top)
    for s in flat:
        f = jnp.exp(s[0:2] - top)
        rest = rest + f * s[2:4]
        first = first + f * s[4:6]
    inverse = 1.0 / (rest + jnp.exp(logit - top))
    label_weight = -rest * inverse
    part = jnp.sum(cot_ref[...] * (first * inverse + label_weight * logit), axis=1, keepdims=True)
    part_ref[...] = jnp.broadcast_to(part[0:1] + part[1:2], part_ref.shape)
    c_own = jnp.exp(mine[0:1] - top[0:1]) * inverse[0:1]
    c_other = jnp.exp(theirs[1:2] - top[0:1]) * inverse[0:1]
    row = lax.broadcasted_iota(jnp.int32, (8, 128), 0)
    stack = jnp.where(row == 0, c_own, jnp.where(row == 1, c_other, label_weight[0:1]))
    coef_ref[...] = pltpu.roll(stack, lax.rem((10 - z) * 16, 128), 1).T


def merge_call(place, cot, up, mid, down):
    return pl.pallas_call(
        merge_kernel,
        in_specs=[smem()] + [vmem()] * 4,
        out_specs=[vmem()] * 2,
        out_shape=[jax.ShapeDtypeStruct((128, 8), jnp.float32), jax.ShapeDtypeStruct((8, 128), jnp.float32)],
        scratch_shapes=[pltpu.VMEM((8, 2, 8, 128), jnp.float32)],
        compiler_params=params(4),
        cost_estimate=pl.CostEstimate(flops=5 * 10**9, bytes_accessed=1024, transcendentals=0),
        name="merge",
    )(place, cot, up, mid, down)


def mix_kernel(coef_ref, o_ref, r_ref, g_ref, gr_ref, pu_ref, pd_ref):
    bf16 = jnp.bfloat16
    half = o_ref.shape[1] // 2
    depth = 2 * half
    for i, (ref, first) in enumerate(((pu_ref, 0), (pu_ref, depth), (None, 0), (pd_ref, 0), (pd_ref, depth))):
        p = mixed(coef_ref, o_ref, r_ref, g_ref, gr_ref, FIRST[i], i, i).astype(bf16)
        if i == 2:
            pu_ref[:, 2 * depth:] = p[:, :half]
            pd_ref[:, 2 * depth:] = p[:, half:]
        else:
            ref[:, first:first + depth] = p


def mixed(coef_ref, o_ref, r_ref, g_ref, gr_ref, k, i, j):
    f32 = jnp.float32
    at, there = slice(16 * k, 16 * k + 16), slice(16 * i, 16 * i + 16)
    label = slice(16 * j, 16 * j + 16)
    c = coef_ref[at, :]
    g = g_ref[at, :].astype(f32) + gr_ref[label, :].astype(f32)
    return c[:, 0:1] * o_ref[at, :] + c[:, 1:2] * r_ref[there, :].astype(f32) + c[:, 2:3] * g


def mix_call(coef, o, r, g, gr):
    depth = g.shape[1]
    bf16 = jnp.bfloat16
    return pl.pallas_call(
        mix_kernel,
        in_specs=[vmem()] * 5,
        out_specs=[vmem()] * 2,
        out_shape=[jax.ShapeDtypeStruct((16, 2 * depth + depth // 2), bf16)] * 2,
        compiler_params=params(8),
        name="mix",
    )(coef, o, r, g, gr)


def rest_kernel(coef_ref, o_ref, r_ref, g_ref, *outs):
    for i, out in enumerate(outs):
        out[...] = mixed(coef_ref, o_ref, r_ref, g_ref, r_ref, SECOND[i], i, i + len(SECOND))


def rest_call(coef, o, r, g):
    depth = g.shape[1]
    return pl.pallas_call(
        rest_kernel,
        in_specs=[vmem()] * 4,
        out_specs=[vmem()] * 3,
        out_shape=[jax.ShapeDtypeStruct((16, depth), jnp.float32)] * 3,
        compiler_params=params(8),
        name="rest",
    )(coef, o, r, g)


def shards(queries, memory, log_scale, labels, valid, cotangent):
    f32, bf16 = jnp.float32, jnp.bfloat16
    together = lambda *arrays: lax.optimization_barrier(arrays)
    scale = jnp.exp(log_scale)
    where = lax.axis_index("mem")
    z = lax.rem(where, 8)
    x_lo = where // 8
    depth = memory.shape[1]
    half = depth // 2
    start_row = where * memory.shape[0]
    roll_by = lax.rem(z + 6, 8) * 16

    up3, down3 = both(queries, queries, 3)
    own_labels = lax.dynamic_slice_in_dim(labels, x_lo * 128, 128)
    own_cot = lax.dynamic_slice_in_dim(cotangent, x_lo * 128, 128)
    rolled = lax.dynamic_slice_in_dim(jnp.concatenate([own_labels, own_labels]), roll_by, 128)
    up3, late_queries = together(up3, queries)
    to_up, to_down, to_x = pack_call(late_queries, up3, down3, rolled[None, :], own_cot[None, :])
    up, down = both(to_up, to_down, 1)
    three_x = send(to_x, PARTNER)
    note = three_x[:, 3 * depth:].astype(f32)
    lab = (jnp.concatenate([rolled, (note[0] * 256.0 + note[1]).astype(jnp.int32)]) - start_row)[:, None]
    cots = jnp.stack([own_cot, (note[2] + note[3]) + note[4]])
    up, down, lab = together(up, down, lab)
    up_x, down_x = send(up, PARTNER), send(down, PARTNER)
    resident, g, g_first, g_second = labels_call(lab, memory)
    resident = pltpu.with_memory_space_constraint(resident, pltpu.VMEM)
    g_first_x = send(g_first, PARTNER)
    blocks = (to_x, up, down, three_x, up_x, down_x)

    e, stat = logits_call(scale, roll_by.reshape(1), blocks, resident, lab, valid[None, :])
    stat_other = send(stat, PARTNER)
    o, o_first, o_second = weighted_call(e, resident, g_second)
    stat_other, o_first, o_second, g_first_x = together(stat_other, o_first, o_second, g_first_x)
    r_first = send(o_first, PARTNER)
    pair = jnp.stack([stat, stat_other])
    s_up, s_down = both(pair, pair, 1)
    three = jnp.stack([s_up, pair, s_down])
    t_up, t_down = both(three, three[:2], 3)
    t_up, t_down, o_second = together(t_up, t_down, o_second)
    coef, part = merge_call(jnp.stack([z, x_lo]), cots, t_up, three, t_down)
    r_second = send(o_second, PARTNER)
    pu, pd = mix_call(coef, o, r_first, g, g_first_x)
    au, ad = both(pu, pd, 1)
    p0, p3, p5 = rest_call(coef, o, r_second, g)
    for pairs in (CROSS, CORE):
        part = part + send(part, pairs)
    au, ad, part, p0, p3, p5 = together(au, ad, part, p0, p3, p5)
    zero = jnp.zeros((16, half), f32)
    near, next_, last = slice(0, depth), slice(depth, 2 * depth), slice(2 * depth, 2 * depth + half)
    p3 = p3 + ad[:, next_].astype(f32) + jnp.concatenate([au[:, last].astype(f32), zero], axis=1)
    p5 = p5 + au[:, next_].astype(f32) + jnp.concatenate([zero, ad[:, last].astype(f32)], axis=1)
    p3, p5, part = together(p3.astype(bf16), p5.astype(bf16), part)
    a3, a5 = both(p3, p5, 3)
    for pairs in (Y1, Y2):
        part = part + send(part, pairs)
    summed = p0 + (au[:, near].astype(f32) + ad[:, near].astype(f32)) + (a3.astype(f32) + a5.astype(f32))
    q_rows = queries.shape[0]
    a3, last_cot = together(a3, cotangent)
    my_cot = lax.dynamic_slice_in_dim(last_cot, where * q_rows, q_rows)
    grad_queries = (scale * my_cot[:, None] * summed).astype(bf16)

    count = cotangent.shape[0] * lax.axis_size("dp")
    scale_grad = part[0, 0:1] / count
    return (grad_queries, scale_grad)


def solution(mesh):
    placed = (P(("dp", "mem"), None), P("mem", None), P(), P("dp"), P("mem"), P("dp"))
    return jax.shard_map(
        shards, mesh=mesh, in_specs=placed, out_specs=(P(("dp", "mem"), None), P()), check_vma=False
    )
```

```python
import jax
import jax.numpy as jnp
from jax import lax
from jax.experimental import pallas as pl
from jax.experimental.pallas import tpu as pltpu
from jax.sharding import PartitionSpec as P

AXES = ("dp", "mem")
NEG = -1e30
BLK = 512
COLS = 1024


def table(move):
    pairs = []
    for y in range(4):
        for x in range(4):
            for c in range(2):
                for z in range(8):
                    index = lambda y, x, c, z: (((y * 2 + x // 2) * 2 + c) * 2 + x % 2) * 8 + z
                    pairs.append((index(y, x, c, z), index(*move(y, x, c, z))))
    return pairs


def along_z(k):
    return table(lambda y, x, c, z: (y, x, c, (z + k) % 8))


def partner_of(x, c):
    if c == 0:
        return x ^ 1
    return (x + 1) % 4 if x % 2 else (x - 1) % 4


PARTNER = table(lambda y, x, c, z: (y, partner_of(x, c), c, z))
CORE = table(lambda y, x, c, z: (y, x, 1 - c, z))
CROSS = table(lambda y, x, c, z: (y, partner_of(x, 1 - c), c, z))
Y1 = table(lambda y, x, c, z: (y ^ 1, x, c, z))
Y2 = table(lambda y, x, c, z: (y ^ 2, x, c, z))


def send(x, pairs):
    return lax.ppermute(x, AXES, pairs)


def both(up, down, k):
    down = send(down, along_z(-k))
    return send(up, along_z(k)), down


def fill(q_scr, first, own, two, up, down):
    depth = q_scr.shape[1]
    half = depth // 2
    near, next_, last = slice(0, depth), slice(depth, 2 * depth), slice(2 * depth, 2 * depth + half)
    places = (down, next_), (up, near), (own, near), (down, near), (up, next_), (two, next_), None, (two, near)
    for k, place in enumerate(places):
        if place is not None:
            q_scr[first + 16 * k:first + 16 * k + 16, :] = place[0][:, place[1]]
    q_scr[first + 96:first + 112, :half] = up[:, last]
    q_scr[first + 96:first + 112, half:] = down[:, last]


def stage_kernel(own_ref, lab_ref, out_ref, sem):
    copy = pltpu.make_async_copy(own_ref, out_ref, sem)
    copy.start()
    copy.wait()


def stage_call(own, lab):
    return pl.pallas_call(
        stage_kernel,
        in_specs=[hbm(), vmem()],
        out_specs=vmem(),
        out_shape=pltpu.VMEM(own.shape, own.dtype),
        scratch_shapes=[pltpu.SemaphoreType.DMA],
        compiler_params=params(4),
        name="stage",
    )(pltpu.with_memory_space_constraint(own, pltpu.HBM), lab)


def pack_kernel(own_ref, up3_ref, down3_ref, lab_ref, cot_ref, up_ref, down_ref, three_ref, two_ref):
    f32, bf16 = jnp.float32, jnp.bfloat16
    depth = up3_ref.shape[1]
    half = depth // 2
    for ref in (up_ref, down_ref, three_ref, two_ref):
        ref[:, :depth] = own_ref[...]
    up_ref[:, depth:2 * depth] = down3_ref[...]
    up_ref[:, 2 * depth:] = up3_ref[:, :half]
    down_ref[:, depth:2 * depth] = up3_ref[...]
    down_ref[:, 2 * depth:] = down3_ref[:, half:]
    two_ref[:, :depth] = up3_ref[...]
    two_ref[:, depth:] = down3_ref[...]
    label = lab_ref[...]
    high = lax.shift_right_logical(label, 8)
    rest = cot_ref[...]
    terms = [high.astype(f32), (label - high * 256).astype(f32)]
    for _ in range(3):
        term = rest.astype(bf16).astype(f32)
        terms.append(term)
        rest = rest - term
    row = lax.broadcasted_iota(jnp.int32, (16, 128), 0)
    note = jnp.zeros((16, 128), f32)
    for k, term in enumerate(terms):
        note = jnp.where(row == k, term, note)
    three_ref[:, depth:] = note.astype(bf16)


def pack_call(own, up3, down3, lab, cot):
    rows, depth = own.shape
    wide = 2 * depth + depth // 2
    return pl.pallas_call(
        pack_kernel,
        in_specs=[vmem()] * 5,
        out_specs=[vmem()] * 4,
        out_shape=[jax.ShapeDtypeStruct((rows, k), jnp.bfloat16) for k in (wide, wide, depth + 128, 2 * depth)],
        compiler_params=params(4),
        name="pack",
    )(own, up3, down3, lab, cot)


def logits_kernel(scale_ref, shift_ref, own, two, up, down, own_x, two_x, up_x, down_x,
                  mem_ref, lab_ref, valid_ref, e_ref, stat_ref, q_scr, l_scr):
    fill(q_scr, 0, own, two, up, down)
    fill(q_scr, 128, own_x, two_x, up_x, down_x)
    rows, n = l_scr.shape
    scale = scale_ref[0]
    top = jnp.full((rows, 1), NEG, jnp.float32)
    picked = jnp.zeros((rows, 1), jnp.float32)
    for i in range(0, n, BLK):
        raw = lax.dot_general(
            q_scr[...], mem_ref[i:i + BLK, :], (((1,), (1,)), ((), ())), preferred_element_type=jnp.float32
        )
        logit = raw * scale
        column = lax.broadcasted_iota(jnp.int32, logit.shape, 1) + i
        hit = lab_ref[...] == column
        kept = jnp.where(jnp.logical_and(valid_ref[:, i:i + BLK] > 0, jnp.logical_not(hit)), logit, NEG)
        l_scr[:, i:i + BLK] = kept
        top = jnp.maximum(top, jnp.max(kept, axis=1, keepdims=True))
        picked = picked + jnp.sum(jnp.where(hit, logit, 0.0), axis=1, keepdims=True)
    half = rows // 2
    step = 32
    lane = lax.broadcasted_iota(jnp.int32, (step, 128), 1)
    tiles = []
    for r in range(0, rows, step):
        m = top[r:r + step]
        val = l_scr[r:r + step, :]
        e = jnp.exp(val - m)
        e_ref[r:r + step, :] = e.astype(jnp.bfloat16)
        s = jnp.sum(e, axis=1, keepdims=True)
        t = jnp.sum(e * val, axis=1, keepdims=True)
        tiles.append(jnp.where(lane == 0, m, jnp.where(lane == 1, s, jnp.where(lane == 2, t, picked[r:r + step]))))
    full = jnp.concatenate(tiles, axis=0)
    own = pltpu.roll(full[:half].T, shift_ref[0], 1)
    other = pltpu.roll(full[half:].T, shift_ref[0], 1)
    for k in range(4):
        stat_ref[2 * k:2 * k + 1, :] = own[k:k + 1, :]
        stat_ref[2 * k + 1:2 * k + 2, :] = other[k:k + 1, :]


def vmem():
    return pl.BlockSpec(memory_space=pltpu.VMEM)


def smem():
    return pl.BlockSpec(memory_space=pltpu.SMEM)


def params(mib):
    return pltpu.CompilerParams(vmem_limit_bytes=mib * 1024 * 1024)


def logits_call(scale, shift, blocks, memory, lab, valid):
    n, depth = memory.shape
    rows = lab.shape[0]
    return pl.pallas_call(
        logits_kernel,
        in_specs=[smem(), smem()] + [vmem()] * (len(blocks) + 3),
        out_specs=[vmem(), vmem()],
        out_shape=[
            jax.ShapeDtypeStruct((rows, n), jnp.bfloat16),
            jax.ShapeDtypeStruct((8, 128), jnp.float32),
        ],
        scratch_shapes=[
            pltpu.VMEM((rows, depth), jnp.bfloat16),
            pltpu.VMEM((rows, n), jnp.float32),
        ],
        compiler_params=params(8),
        cost_estimate=pl.CostEstimate(
            flops=2 * rows * n * depth, bytes_accessed=2 * n * depth, transcendentals=rows * n
        ),
        name="logits",
    )(scale, shift, *blocks, memory, lab, valid)


FIRST = (3, 0, 6, 1, 4)
SECOND = (2, 5, 7)


def weighted_kernel(e_ref, mem_ref, g_ref, own_ref, first_ref, second_ref):
    second_ref[16 * len(SECOND):, :] = g_ref[...]
    for c in range(0, mem_ref.shape[1], COLS):
        at = slice(c, c + COLS)
        out = jnp.dot(e_ref[...], mem_ref[:, at], preferred_element_type=jnp.float32)
        spread(out, at, own_ref, first_ref, second_ref)


def spread(out, at, own_ref, first_ref, second_ref):
    own_ref[:, at] = out[:128].astype(own_ref.dtype)
    for ref, order in ((first_ref, FIRST), (second_ref, SECOND)):
        for i, k in enumerate(order):
            ref[16 * i:16 * i + 16, at] = out[128 + 16 * k:144 + 16 * k].astype(ref.dtype)


def weighted_call(e, memory, g):
    rows, n = e.shape
    depth = memory.shape[1]
    return pl.pallas_call(
        weighted_kernel,
        in_specs=[vmem()] * 3,
        out_specs=[vmem()] * 3,
        out_shape=[
            jax.ShapeDtypeStruct((128, depth), jnp.float32),
            jax.ShapeDtypeStruct((16 * len(FIRST), depth), jnp.bfloat16),
            jax.ShapeDtypeStruct((32 * len(SECOND), depth), jnp.bfloat16),
        ],
        compiler_params=params(8),
        cost_estimate=pl.CostEstimate(flops=2 * rows * n * depth, bytes_accessed=2 * n * depth, transcendentals=0),
        name="weighted",
    )(e, memory, g)


def labels_kernel(lab_ref, mem_ref, copy_ref, own_ref, first_ref, second_ref, hit_scr, sems):
    rows, n = hit_scr.shape
    pieces = mem_ref.shape[1] // COLS

    def piece(k):
        at = pl.ds(k * COLS, COLS)
        return pltpu.make_async_copy(mem_ref.at[:, at], copy_ref.at[:, at], sems.at[k])

    for k in range(pieces):
        piece(k).start()
    for i in range(0, n, BLK):
        column = lax.broadcasted_iota(jnp.int32, (rows, BLK), 1) + i
        hit_scr[:, i:i + BLK] = jnp.where(lab_ref[...] == column, 1.0, 0.0).astype(jnp.bfloat16)
    for k in range(pieces):
        piece(k).wait()
        at = slice(k * COLS, k * COLS + COLS)
        out = jnp.dot(hit_scr[...], copy_ref[:, at], preferred_element_type=jnp.float32)
        spread(out, at, own_ref, first_ref, second_ref)


def hbm():
    return pl.BlockSpec(memory_space=pltpu.HBM)


def labels_call(lab, memory):
    rows = lab.shape[0]
    n, depth = memory.shape
    return pl.pallas_call(
        labels_kernel,
        in_specs=[vmem(), hbm()],
        out_specs=[vmem()] * 4,
        out_shape=[
            pltpu.VMEM((n, depth), jnp.bfloat16),
            jax.ShapeDtypeStruct((128, depth), jnp.bfloat16),
            jax.ShapeDtypeStruct((16 * len(FIRST), depth), jnp.bfloat16),
            jax.ShapeDtypeStruct((16 * len(SECOND), depth), jnp.bfloat16),
        ],
        scratch_shapes=[pltpu.VMEM((rows, n), jnp.bfloat16), pltpu.SemaphoreType.DMA((depth // COLS,))],
        compiler_params=params(8),
        cost_estimate=pl.CostEstimate(flops=1024, bytes_accessed=1024, transcendentals=0),
        name="label_rows",
    )(lab, pltpu.with_memory_space_constraint(memory, pltpu.HBM))


def merge_kernel(place_ref, cot_ref, up_ref, mid_ref, down_ref, coef_ref, part_ref, sets):
    z, x_lo = place_ref[0], place_ref[1]
    sets[0:3] = up_ref[...]
    sets[3:6] = mid_ref[...]
    sets[6:8] = down_ref[...]
    mine, theirs = sets[4, 0], sets[4, 1]
    flat = []
    for a in range(8):
        at = lax.rem(a - z + 12, 8)
        own, other = sets[at, 0], sets[at, 1]
        row = lax.broadcasted_iota(jnp.int32, other.shape, 0)
        swapped = jnp.where(row % 2 == 0, pltpu.roll(other, 7, 0), pltpu.roll(other, 1, 0))
        is_low = x_lo == 0
        flat += [jnp.where(is_low, own, swapped), jnp.where(is_low, swapped, own)]
    top = flat[0][0:2]
    logit = jnp.zeros_like(top)
    for s in flat:
        top = jnp.maximum(top, s[0:2])
        logit = logit + s[6:8]
    top = jnp.maximum(top, logit)
    rest = jnp.zeros_like(top)
    first = jnp.zeros_like(top)
    for s in flat:
        f = jnp.exp(s[0:2] - top)
        rest = rest + f * s[2:4]
        first = first + f * s[4:6]
    inverse = 1.0 / (rest + jnp.exp(logit - top))
    label_weight = -rest * inverse
    part = jnp.sum(cot_ref[...] * (first * inverse + label_weight * logit), axis=1, keepdims=True)
    part_ref[...] = jnp.broadcast_to(part[0:1] + part[1:2], part_ref.shape)
    c_own = jnp.exp(mine[0:1] - top[0:1]) * inverse[0:1]
    c_other = jnp.exp(theirs[1:2] - top[0:1]) * inverse[0:1]
    row = lax.broadcasted_iota(jnp.int32, (8, 128), 0)
    stack = jnp.where(row == 0, c_own, jnp.where(row == 1, c_other, label_weight[0:1]))
    coef_ref[...] = pltpu.roll(stack, lax.rem((10 - z) * 16, 128), 1).T


def merge_call(place, cot, up, mid, down):
    return pl.pallas_call(
        merge_kernel,
        in_specs=[smem()] + [vmem()] * 4,
        out_specs=[vmem()] * 2,
        out_shape=[jax.ShapeDtypeStruct((128, 8), jnp.float32), jax.ShapeDtypeStruct((8, 128), jnp.float32)],
        scratch_shapes=[pltpu.VMEM((8, 2, 8, 128), jnp.float32)],
        compiler_params=params(4),
        cost_estimate=pl.CostEstimate(flops=5 * 10**9, bytes_accessed=1024, transcendentals=0),
        name="merge",
    )(place, cot, up, mid, down)


def mix_kernel(coef_ref, o_ref, r_ref, g_ref, gr_ref, pu_ref, pd_ref):
    bf16 = jnp.bfloat16
    half = o_ref.shape[1] // 2
    depth = 2 * half
    for i, (ref, first) in enumerate(((pu_ref, 0), (pu_ref, depth), (None, 0), (pd_ref, 0), (pd_ref, depth))):
        p = mixed(coef_ref, o_ref, r_ref, g_ref, gr_ref, FIRST[i], i, i).astype(bf16)
        if i == 2:
            pu_ref[:, 2 * depth:] = p[:, :half]
            pd_ref[:, 2 * depth:] = p[:, half:]
        else:
            ref[:, first:first + depth] = p


def mixed(coef_ref, o_ref, r_ref, g_ref, gr_ref, k, i, j):
    f32 = jnp.float32
    at, there = slice(16 * k, 16 * k + 16), slice(16 * i, 16 * i + 16)
    label = slice(16 * j, 16 * j + 16)
    c = coef_ref[at, :]
    g = g_ref[at, :].astype(f32) + gr_ref[label, :].astype(f32)
    return c[:, 0:1] * o_ref[at, :] + c[:, 1:2] * r_ref[there, :].astype(f32) + c[:, 2:3] * g


def mix_call(coef, o, r, g, gr):
    depth = g.shape[1]
    bf16 = jnp.bfloat16
    return pl.pallas_call(
        mix_kernel,
        in_specs=[vmem()] * 5,
        out_specs=[vmem()] * 2,
        out_shape=[jax.ShapeDtypeStruct((16, 2 * depth + depth // 2), bf16)] * 2,
        compiler_params=params(8),
        name="mix",
    )(coef, o, r, g, gr)


def rest_kernel(coef_ref, o_ref, r_ref, g_ref, *outs):
    for i, out in enumerate(outs):
        out[...] = mixed(coef_ref, o_ref, r_ref, g_ref, r_ref, SECOND[i], i, i + len(SECOND))


def rest_call(coef, o, r, g):
    depth = g.shape[1]
    return pl.pallas_call(
        rest_kernel,
        in_specs=[vmem()] * 4,
        out_specs=[vmem()] * 3,
        out_shape=[jax.ShapeDtypeStruct((16, depth), jnp.float32)] * 3,
        compiler_params=params(8),
        name="rest",
    )(coef, o, r, g)


def shards(queries, memory, log_scale, labels, valid, cotangent):
    f32, bf16 = jnp.float32, jnp.bfloat16
    together = lambda *arrays: lax.optimization_barrier(arrays)
    scale = jnp.exp(log_scale)
    where = lax.axis_index("mem")
    z = lax.rem(where, 8)
    x_lo = where // 8
    depth = memory.shape[1]
    half = depth // 2
    start_row = where * memory.shape[0]
    roll_by = lax.rem(z + 6, 8) * 16

    up3, down3 = both(queries, queries, 3)
    own_labels = lax.dynamic_slice_in_dim(labels, x_lo * 128, 128)
    own_cot = lax.dynamic_slice_in_dim(cotangent, x_lo * 128, 128)
    rolled = lax.dynamic_slice_in_dim(jnp.concatenate([own_labels, own_labels]), roll_by, 128)
    staged = stage_call(queries, rolled[None, :])
    up3, staged = together(up3, staged)
    to_up, to_down, to_x, to_x2 = pack_call(staged, up3, down3, rolled[None, :], own_cot[None, :])
    up, down = both(to_up, to_down, 1)
    three_x = send(to_x, PARTNER)
    two_x = send(to_x2, PARTNER)
    up, down, three_x, two_x = together(up, down, three_x, two_x)
    note = three_x[:, depth:].astype(f32)
    lab = (jnp.concatenate([rolled, (note[0] * 256.0 + note[1]).astype(jnp.int32)]) - start_row)[:, None]
    cots = jnp.stack([own_cot, (note[2] + note[3]) + note[4]])
    up_x, down_x = send(up, PARTNER), send(down, PARTNER)
    resident, g, g_first, g_second = labels_call(lab, memory)
    resident = pltpu.with_memory_space_constraint(resident, pltpu.VMEM)
    g_first_x = send(g_first, PARTNER)
    blocks = (to_x, to_x2, up, down, three_x, two_x, up_x, down_x)

    e, stat = logits_call(scale, roll_by.reshape(1), blocks, resident, lab, valid[None, :])
    stat_other = send(stat, PARTNER)
    o, o_first, o_second = weighted_call(e, resident, g_second)
    stat_other, o_first, o_second, g_first_x = together(stat_other, o_first, o_second, g_first_x)
    r_first = send(o_first, PARTNER)
    pair = jnp.stack([stat, stat_other])
    s_up, s_down = both(pair, pair, 1)
    three = jnp.stack([s_up, pair, s_down])
    t_up, t_down = both(three, three[:2], 3)
    t_up, t_down, o_second = together(t_up, t_down, o_second)
    coef, part = merge_call(jnp.stack([z, x_lo]), cots, t_up, three, t_down)
    r_second = send(o_second, PARTNER)
    pu, pd = mix_call(coef, o, r_first, g, g_first_x)
    au, ad = both(pu, pd, 1)
    p0, p3, p5 = rest_call(coef, o, r_second, g)
    for pairs in (CROSS, CORE):
        part = part + send(part, pairs)
    au, ad, part, p0, p3, p5 = together(au, ad, part, p0, p3, p5)
    zero = jnp.zeros((16, half), f32)
    near, next_, last = slice(0, depth), slice(depth, 2 * depth), slice(2 * depth, 2 * depth + half)
    p3 = p3 + ad[:, next_].astype(f32) + jnp.concatenate([au[:, last].astype(f32), zero], axis=1)
    p5 = p5 + au[:, next_].astype(f32) + jnp.concatenate([zero, ad[:, last].astype(f32)], axis=1)
    p3, p5, part = together(p3.astype(bf16), p5.astype(bf16), part)
    a3, a5 = both(p3, p5, 3)
    for pairs in (Y1, Y2):
        part = part + send(part, pairs)
    summed = p0 + (au[:, near].astype(f32) + ad[:, near].astype(f32)) + (a3.astype(f32) + a5.astype(f32))
    q_rows = queries.shape[0]
    a3, last_cot = together(a3, cotangent)
    my_cot = lax.dynamic_slice_in_dim(last_cot, where * q_rows, q_rows)
    grad_queries = (scale * my_cot[:, None] * summed).astype(bf16)

    count = cotangent.shape[0] * lax.axis_size("dp")
    scale_grad = part[0, 0:1] / count
    return (grad_queries, scale_grad)


def solution(mesh):
    placed = (P(("dp", "mem"), None), P("mem", None), P(), P("dp"), P("mem"), P("dp"))
    return jax.shard_map(
        shards, mesh=mesh, in_specs=placed, out_specs=(P(("dp", "mem"), None), P()), check_vma=False
    )
```

```python
import functools

import jax
import jax.numpy as jnp
from jax import lax
from jax.experimental import pallas as pl
from jax.experimental.pallas import tpu as pltpu
from jax.sharding import PartitionSpec as P

AXES = ("dp", "mem")
NEG = -1e30
BLK = 512
COLS = 1024


def table(move):
    pairs = []
    for y in range(4):
        for x in range(4):
            for c in range(2):
                for z in range(8):
                    index = lambda y, x, c, z: (((y * 2 + x // 2) * 2 + c) * 2 + x % 2) * 8 + z
                    pairs.append((index(y, x, c, z), index(*move(y, x, c, z))))
    return pairs


def along_z(k):
    return table(lambda y, x, c, z: (y, x, c, (z + k) % 8))


def partner_of(x, c):
    if c == 0:
        return x ^ 1
    return (x + 1) % 4 if x % 2 else (x - 1) % 4


PARTNER = table(lambda y, x, c, z: (y, partner_of(x, c), c, z))
CORE = table(lambda y, x, c, z: (y, x, 1 - c, z))
CROSS = table(lambda y, x, c, z: (y, partner_of(x, 1 - c), c, z))
Y1 = table(lambda y, x, c, z: (y ^ 1, x, c, z))
Y3 = table(lambda y, x, c, z: (y ^ 3, x, c, z))
Y2 = table(lambda y, x, c, z: (y ^ 2, x, c, z))


def send(x, pairs):
    return lax.ppermute(x, AXES, pairs)


def both(up, down, k):
    down = send(down, along_z(-k))
    return send(up, along_z(k)), down


def fill(q_scr, first, own, two, up, down):
    depth = q_scr.shape[1]
    half = depth // 2
    near, next_, last = slice(0, depth), slice(depth, 2 * depth), slice(2 * depth, 2 * depth + half)
    places = (down, next_), (up, near), (own, near), (down, near), (up, next_), (two, next_), None, (two, near)
    for k, place in enumerate(places):
        if place is not None:
            q_scr[first + 16 * k:first + 16 * k + 16, :] = place[0][:, place[1]]
    q_scr[first + 96:first + 112, :half] = up[:, last]
    q_scr[first + 96:first + 112, half:] = down[:, last]


def stage_kernel(own_ref, lab_ref, out_ref, sem):
    copy = pltpu.make_async_copy(own_ref, out_ref, sem)
    copy.start()
    copy.wait()


def stage_call(own, lab):
    return pl.pallas_call(
        stage_kernel,
        in_specs=[hbm(), vmem()],
        out_specs=vmem(),
        out_shape=pltpu.VMEM(own.shape, own.dtype),
        scratch_shapes=[pltpu.SemaphoreType.DMA],
        compiler_params=params(4),
        name="stage",
    )(pltpu.with_memory_space_constraint(own, pltpu.HBM), lab)


def pack_kernel(own_ref, up3_ref, down3_ref, lab_ref, cot_ref, up_ref, down_ref, three_ref, two_ref):
    f32, bf16 = jnp.float32, jnp.bfloat16
    depth = up3_ref.shape[1]
    half = depth // 2
    for ref in (up_ref, down_ref, three_ref, two_ref):
        ref[:, :depth] = own_ref[...]
    up_ref[:, depth:2 * depth] = down3_ref[...]
    up_ref[:, 2 * depth:] = up3_ref[:, :half]
    down_ref[:, depth:2 * depth] = up3_ref[...]
    down_ref[:, 2 * depth:] = down3_ref[:, half:]
    two_ref[:, :depth] = up3_ref[...]
    two_ref[:, depth:] = down3_ref[...]
    label = lab_ref[...]
    high = lax.shift_right_logical(label, 8)
    rest = cot_ref[...]
    terms = [high.astype(f32), (label - high * 256).astype(f32)]
    for _ in range(3):
        term = rest.astype(bf16).astype(f32)
        terms.append(term)
        rest = rest - term
    row = lax.broadcasted_iota(jnp.int32, (16, 128), 0)
    note = jnp.zeros((16, 128), f32)
    for k, term in enumerate(terms):
        note = jnp.where(row == k, term, note)
    three_ref[:, depth:] = note.astype(bf16)


def pack_call(own, up3, down3, lab, cot):
    rows, depth = own.shape
    wide = 2 * depth + depth // 2
    return pl.pallas_call(
        pack_kernel,
        in_specs=[vmem()] * 5,
        out_specs=[vmem()] * 4,
        out_shape=[jax.ShapeDtypeStruct((rows, k), jnp.bfloat16) for k in (wide, wide, depth + 128, 2 * depth)],
        compiler_params=params(4),
        name="pack",
    )(own, up3, down3, lab, cot)


def logits_kernel(scale_ref, shift_ref, own, two, up, down, own_x, two_x, up_x, down_x,
                  mem_ref, lab_ref, valid_ref, e_ref, stat_ref, q_scr, l_scr):
    fill(q_scr, 0, own, two, up, down)
    fill(q_scr, 128, own_x, two_x, up_x, down_x)
    rows, n = l_scr.shape
    scale = scale_ref[0]
    top = jnp.full((rows, 1), NEG, jnp.float32)
    picked = jnp.zeros((rows, 1), jnp.float32)
    for i in range(0, n, BLK):
        raw = lax.dot_general(
            q_scr[...], mem_ref[i:i + BLK, :], (((1,), (1,)), ((), ())), preferred_element_type=jnp.float32
        )
        logit = raw * scale
        column = lax.broadcasted_iota(jnp.int32, logit.shape, 1) + i
        hit = lab_ref[...] == column
        kept = jnp.where(jnp.logical_and(valid_ref[:, i:i + BLK] > 0, jnp.logical_not(hit)), logit, NEG)
        l_scr[:, i:i + BLK] = kept
        top = jnp.maximum(top, jnp.max(kept, axis=1, keepdims=True))
        picked = picked + jnp.sum(jnp.where(hit, logit, 0.0), axis=1, keepdims=True)
    half = rows // 2
    step = 32
    lane = lax.broadcasted_iota(jnp.int32, (step, 128), 1)
    tiles = []
    for r in range(0, rows, step):
        m = top[r:r + step]
        val = l_scr[r:r + step, :]
        e = jnp.exp(val - m)
        e_ref[r:r + step, :] = e.astype(jnp.bfloat16)
        s = jnp.sum(e, axis=1, keepdims=True)
        t = jnp.sum(e * val, axis=1, keepdims=True)
        tiles.append(jnp.where(lane == 0, m, jnp.where(lane == 1, s, jnp.where(lane == 2, t, picked[r:r + step]))))
    full = jnp.concatenate(tiles, axis=0)
    own = pltpu.roll(full[:half].T, shift_ref[0], 1)
    other = pltpu.roll(full[half:].T, shift_ref[0], 1)
    for k in range(4):
        stat_ref[2 * k:2 * k + 1, :] = own[k:k + 1, :]
        stat_ref[2 * k + 1:2 * k + 2, :] = other[k:k + 1, :]


def vmem():
    return pl.BlockSpec(memory_space=pltpu.VMEM)


def smem():
    return pl.BlockSpec(memory_space=pltpu.SMEM)


def params(mib):
    return pltpu.CompilerParams(vmem_limit_bytes=mib * 1024 * 1024)


def logits_call(scale, shift, blocks, memory, lab, valid):
    n, depth = memory.shape
    rows = lab.shape[0]
    return pl.pallas_call(
        logits_kernel,
        in_specs=[smem(), smem()] + [vmem()] * (len(blocks) + 3),
        out_specs=[vmem(), vmem()],
        out_shape=[
            jax.ShapeDtypeStruct((rows, n), jnp.bfloat16),
            jax.ShapeDtypeStruct((8, 128), jnp.float32),
        ],
        scratch_shapes=[
            pltpu.VMEM((rows, depth), jnp.bfloat16),
            pltpu.VMEM((rows, n), jnp.float32),
        ],
        compiler_params=params(8),
        cost_estimate=pl.CostEstimate(
            flops=2 * rows * n * depth, bytes_accessed=2 * n * depth, transcendentals=rows * n
        ),
        name="logits",
    )(scale, shift, *blocks, memory, lab, valid)


FIRST = (3, 0, 6, 1, 4)
SECOND = (2, 5, 7)


def weighted_kernel(e_ref, mem_ref, g_ref, own_ref, first_ref, second_ref):
    second_ref[16 * len(SECOND):, :] = g_ref[...]
    for c in range(0, mem_ref.shape[1], COLS):
        at = slice(c, c + COLS)
        out = jnp.dot(e_ref[...], mem_ref[:, at], preferred_element_type=jnp.float32)
        spread(out, at, own_ref, first_ref, second_ref)


def spread(out, at, own_ref, first_ref, second_ref):
    own_ref[:, at] = out[:128].astype(own_ref.dtype)
    for ref, order in ((first_ref, FIRST), (second_ref, SECOND)):
        for i, k in enumerate(order):
            ref[16 * i:16 * i + 16, at] = out[128 + 16 * k:144 + 16 * k].astype(ref.dtype)


def weighted_call(e, memory, g):
    rows, n = e.shape
    depth = memory.shape[1]
    return pl.pallas_call(
        weighted_kernel,
        in_specs=[vmem()] * 3,
        out_specs=[vmem()] * 3,
        out_shape=[
            jax.ShapeDtypeStruct((128, depth), jnp.float32),
            jax.ShapeDtypeStruct((16 * len(FIRST), depth), jnp.bfloat16),
            jax.ShapeDtypeStruct((32 * len(SECOND), depth), jnp.bfloat16),
        ],
        compiler_params=params(8),
        cost_estimate=pl.CostEstimate(flops=2 * rows * n * depth, bytes_accessed=2 * n * depth, transcendentals=0),
        name="weighted",
    )(e, memory, g)


def labels_kernel(lab_ref, mem_ref, copy_ref, own_ref, first_ref, second_ref, hit_scr, sems):
    rows, n = hit_scr.shape
    pieces = mem_ref.shape[1] // COLS

    def piece(k):
        at = pl.ds(k * COLS, COLS)
        return pltpu.make_async_copy(mem_ref.at[:, at], copy_ref.at[:, at], sems.at[k])

    for k in range(pieces):
        piece(k).start()
    for i in range(0, n, BLK):
        column = lax.broadcasted_iota(jnp.int32, (rows, BLK), 1) + i
        hit_scr[:, i:i + BLK] = jnp.where(lab_ref[...] == column, 1.0, 0.0).astype(jnp.bfloat16)
    for k in range(pieces):
        piece(k).wait()
        at = slice(k * COLS, k * COLS + COLS)
        out = jnp.dot(hit_scr[...], copy_ref[:, at], preferred_element_type=jnp.float32)
        spread(out, at, own_ref, first_ref, second_ref)


def hbm():
    return pl.BlockSpec(memory_space=pltpu.HBM)


def labels_call(lab, memory):
    rows = lab.shape[0]
    n, depth = memory.shape
    return pl.pallas_call(
        labels_kernel,
        in_specs=[vmem(), hbm()],
        out_specs=[vmem()] * 4,
        out_shape=[
            pltpu.VMEM((n, depth), jnp.bfloat16),
            jax.ShapeDtypeStruct((128, depth), jnp.bfloat16),
            jax.ShapeDtypeStruct((16 * len(FIRST), depth), jnp.bfloat16),
            jax.ShapeDtypeStruct((16 * len(SECOND), depth), jnp.bfloat16),
        ],
        scratch_shapes=[pltpu.VMEM((rows, n), jnp.bfloat16), pltpu.SemaphoreType.DMA((depth // COLS,))],
        compiler_params=params(8),
        cost_estimate=pl.CostEstimate(flops=1024, bytes_accessed=1024, transcendentals=0),
        name="label_rows",
    )(lab, pltpu.with_memory_space_constraint(memory, pltpu.HBM))


def merge_kernel(place_ref, cot_ref, up_ref, mid_ref, down_ref, coef_ref, part_ref, sets):
    z, x_lo = place_ref[0], place_ref[1]
    sets[0:3] = up_ref[...]
    sets[3:6] = mid_ref[...]
    sets[6:8] = down_ref[...]
    mine, theirs = sets[4, 0], sets[4, 1]
    flat = []
    for a in range(8):
        at = lax.rem(a - z + 12, 8)
        own, other = sets[at, 0], sets[at, 1]
        row = lax.broadcasted_iota(jnp.int32, other.shape, 0)
        swapped = jnp.where(row % 2 == 0, pltpu.roll(other, 7, 0), pltpu.roll(other, 1, 0))
        is_low = x_lo == 0
        flat += [jnp.where(is_low, own, swapped), jnp.where(is_low, swapped, own)]
    top = flat[0][0:2]
    logit = jnp.zeros_like(top)
    for s in flat:
        top = jnp.maximum(top, s[0:2])
        logit = logit + s[6:8]
    top = jnp.maximum(top, logit)
    rest = jnp.zeros_like(top)
    first = jnp.zeros_like(top)
    for s in flat:
        f = jnp.exp(s[0:2] - top)
        rest = rest + f * s[2:4]
        first = first + f * s[4:6]
    inverse = 1.0 / (rest + jnp.exp(logit - top))
    label_weight = -rest * inverse
    part = jnp.sum(cot_ref[...] * (first * inverse + label_weight * logit), axis=1, keepdims=True)
    part_ref[...] = jnp.broadcast_to(part[0:1] + part[1:2], part_ref.shape)
    c_own = jnp.exp(mine[0:1] - top[0:1]) * inverse[0:1]
    c_other = jnp.exp(theirs[1:2] - top[0:1]) * inverse[0:1]
    row = lax.broadcasted_iota(jnp.int32, (8, 128), 0)
    stack = jnp.where(row == 0, c_own, jnp.where(row == 1, c_other, label_weight[0:1]))
    coef_ref[...] = pltpu.roll(stack, lax.rem((10 - z) * 16, 128), 1).T


def merge_call(place, cot, up, mid, down):
    return pl.pallas_call(
        merge_kernel,
        in_specs=[smem()] + [vmem()] * 4,
        out_specs=[vmem()] * 2,
        out_shape=[jax.ShapeDtypeStruct((128, 8), jnp.float32), jax.ShapeDtypeStruct((8, 128), jnp.float32)],
        scratch_shapes=[pltpu.VMEM((8, 2, 8, 128), jnp.float32)],
        compiler_params=params(4),
        cost_estimate=pl.CostEstimate(flops=5 * 10**9, bytes_accessed=1024, transcendentals=0),
        name="merge",
    )(place, cot, up, mid, down)


def mix_kernel(coef_ref, o_ref, r_ref, g_ref, gr_ref, pu_ref, pd_ref):
    bf16 = jnp.bfloat16
    half = o_ref.shape[1] // 2
    depth = 2 * half
    for i, (ref, first) in enumerate(((pu_ref, 0), (pu_ref, depth), (None, 0), (pd_ref, 0), (pd_ref, depth))):
        p = mixed(coef_ref, o_ref, r_ref, g_ref, gr_ref, FIRST[i], i, i).astype(bf16)
        if i == 2:
            pu_ref[:, 2 * depth:] = p[:, :half]
            pd_ref[:, 2 * depth:] = p[:, half:]
        else:
            ref[:, first:first + depth] = p


def mixed(coef_ref, o_ref, r_ref, g_ref, gr_ref, k, i, j):
    f32 = jnp.float32
    at, there = slice(16 * k, 16 * k + 16), slice(16 * i, 16 * i + 16)
    label = slice(16 * j, 16 * j + 16)
    c = coef_ref[at, :]
    g = g_ref[at, :].astype(f32) + gr_ref[label, :].astype(f32)
    return c[:, 0:1] * o_ref[at, :] + c[:, 1:2] * r_ref[there, :].astype(f32) + c[:, 2:3] * g


def mix_call(coef, o, r, g, gr):
    depth = g.shape[1]
    bf16 = jnp.bfloat16
    return pl.pallas_call(
        mix_kernel,
        in_specs=[vmem()] * 5,
        out_specs=[vmem()] * 2,
        out_shape=[jax.ShapeDtypeStruct((16, 2 * depth + depth // 2), bf16)] * 2,
        compiler_params=params(8),
        name="mix",
    )(coef, o, r, g, gr)


def rest_kernel(coef_ref, o_ref, r_ref, g_ref, *outs):
    for i, out in enumerate(outs):
        out[...] = mixed(coef_ref, o_ref, r_ref, g_ref, r_ref, SECOND[i], i, i + len(SECOND))


def rest_call(coef, o, r, g):
    depth = g.shape[1]
    return pl.pallas_call(
        rest_kernel,
        in_specs=[vmem()] * 4,
        out_specs=[vmem()] * 3,
        out_shape=[jax.ShapeDtypeStruct((16, depth), jnp.float32)] * 3,
        compiler_params=params(8),
        name="rest",
    )(coef, o, r, g)


def final_kernel(count, factor_ref, p0_ref, au_ref, ad_ref, a3_ref, a5_ref, s0, s2, s1, s3, out_ref, sum_ref):
    f32 = jnp.float32
    depth = out_ref.shape[1]
    for c in range(0, depth, 512):
        at = slice(c, c + 512)
        near = au_ref[:, at].astype(f32) + ad_ref[:, at].astype(f32)
        wide = a3_ref[:, at].astype(f32) + a5_ref[:, at].astype(f32)
        out_ref[:, at] = (factor_ref[...] * (p0_ref[:, at] + near + wide)).astype(out_ref.dtype)


    total = ((s0[...] + s2[...]) + (s1[...] + s3[...])) / count
    sum_ref[0] = total[0, 0]


def final_call(count, factor, p0, au, ad, a3, a5, *parts):
    return pl.pallas_call(
        functools.partial(final_kernel, count),
        in_specs=[vmem()] * 10,
        out_specs=[vmem(), smem()],
        out_shape=[jax.ShapeDtypeStruct(a3.shape, a3.dtype), jax.ShapeDtypeStruct((1,), jnp.float32)],
        compiler_params=params(4),
        cost_estimate=pl.CostEstimate(flops=5 * 10**9, bytes_accessed=1024, transcendentals=0),
        name="final",
    )(factor, p0, au, ad, a3, a5, *parts)


def shards(queries, memory, log_scale, labels, valid, cotangent):
    f32, bf16 = jnp.float32, jnp.bfloat16
    together = lambda *arrays: lax.optimization_barrier(arrays)
    scale = jnp.exp(log_scale)
    where = lax.axis_index("mem")
    z = lax.rem(where, 8)
    x_lo = where // 8
    depth = memory.shape[1]
    half = depth // 2
    start_row = where * memory.shape[0]
    roll_by = lax.rem(z + 6, 8) * 16

    up3, down3 = both(queries, queries, 3)
    own_labels = lax.dynamic_slice_in_dim(labels, x_lo * 128, 128)
    own_cot = lax.dynamic_slice_in_dim(cotangent, x_lo * 128, 128)
    rolled = lax.dynamic_slice_in_dim(jnp.concatenate([own_labels, own_labels]), roll_by, 128)
    staged = stage_call(queries, rolled[None, :])
    up3, staged = together(up3, staged)
    to_up, to_down, to_x, to_x2 = pack_call(staged, up3, down3, rolled[None, :], own_cot[None, :])
    up, down = both(to_up, to_down, 1)
    three_x = send(to_x, PARTNER)
    two_x = send(to_x2, PARTNER)
    up, down, three_x, two_x = together(up, down, three_x, two_x)
    note = three_x[:, depth:].astype(f32)
    lab = (jnp.concatenate([rolled, (note[0] * 256.0 + note[1]).astype(jnp.int32)]) - start_row)[:, None]
    cots = jnp.stack([own_cot, (note[2] + note[3]) + note[4]])
    up_x, down_x = send(up, PARTNER), send(down, PARTNER)
    resident, g, g_first, g_second = labels_call(lab, memory)
    resident = pltpu.with_memory_space_constraint(resident, pltpu.VMEM)
    g_first_x = send(g_first, PARTNER)
    blocks = (to_x, to_x2, up, down, three_x, two_x, up_x, down_x)

    e, stat = logits_call(scale, roll_by.reshape(1), blocks, resident, lab, valid[None, :])
    stat_other = send(stat, PARTNER)
    o, o_first, o_second = weighted_call(e, resident, g_second)
    stat_other, o_first, o_second, g_first_x = together(stat_other, o_first, o_second, g_first_x)
    r_first = send(o_first, PARTNER)
    pair = jnp.stack([stat, stat_other])
    s_up, s_down = both(pair, pair, 1)
    s_up, o_second = together(s_up, o_second)
    three = jnp.stack([s_up, pair, s_down])
    t_up, t_down = both(three, three[:2], 3)
    coef, part = merge_call(jnp.stack([z, x_lo]), cots, t_up, three, t_down)
    r_second = send(o_second, PARTNER)
    pu, pd = mix_call(coef, o, r_first, g, g_first_x)
    au, ad = both(pu, pd, 1)
    p0, p3, p5 = rest_call(coef, o, r_second, g)
    for pairs in (CROSS, CORE):
        part = part + send(part, pairs)
    au, ad, part, p0, p3, p5 = together(au, ad, part, p0, p3, p5)
    zero = jnp.zeros((16, half), f32)
    near, next_, last = slice(0, depth), slice(depth, 2 * depth), slice(2 * depth, 2 * depth + half)
    p3 = p3 + ad[:, next_].astype(f32) + jnp.concatenate([au[:, last].astype(f32), zero], axis=1)
    p5 = p5 + au[:, next_].astype(f32) + jnp.concatenate([zero, ad[:, last].astype(f32)], axis=1)
    p3, p5, part = together(p3.astype(bf16), p5.astype(bf16), part)
    a3, a5 = both(p3, p5, 3)
    parts = part, send(part, Y2), send(part, Y1), send(part, Y3)
    q_rows = queries.shape[0]
    my_cot = lax.dynamic_slice_in_dim(cotangent, where * q_rows, q_rows)
    count = cotangent.shape[0] * lax.axis_size("dp")
    return final_call(count, (scale * my_cot)[:, None], p0, au, ad, a3, a5, *parts)


def solution(mesh):
    placed = (P(("dp", "mem"), None), P("mem", None), P(), P("dp"), P("mem"), P("dp"))
    return jax.shard_map(
        shards, mesh=mesh, in_specs=placed, out_specs=(P(("dp", "mem"), None), P()), check_vma=False
    )
```

```python
import functools

import jax
import jax.numpy as jnp
from jax import lax
from jax.experimental import pallas as pl
from jax.experimental.pallas import tpu as pltpu
from jax.sharding import PartitionSpec as P

AXES = ("dp", "mem")
NEG = -1e30
BLK = 512
COLS = 1024


def table(move):
    pairs = []
    for y in range(4):
        for x in range(4):
            for c in range(2):
                for z in range(8):
                    index = lambda y, x, c, z: (((y * 2 + x // 2) * 2 + c) * 2 + x % 2) * 8 + z
                    pairs.append((index(y, x, c, z), index(*move(y, x, c, z))))
    return pairs


def along_z(k):
    return table(lambda y, x, c, z: (y, x, c, (z + k) % 8))


def partner_of(x, c):
    if c == 0:
        return x ^ 1
    return (x + 1) % 4 if x % 2 else (x - 1) % 4


PARTNER = table(lambda y, x, c, z: (y, partner_of(x, c), c, z))
CORE = table(lambda y, x, c, z: (y, x, 1 - c, z))
CROSS = table(lambda y, x, c, z: (y, partner_of(x, 1 - c), c, z))
Y1 = table(lambda y, x, c, z: (y ^ 1, x, c, z))
Y3 = table(lambda y, x, c, z: (y ^ 3, x, c, z))
Y2 = table(lambda y, x, c, z: (y ^ 2, x, c, z))


def send(x, pairs):
    return lax.ppermute(x, AXES, pairs)


def both(up, down, k):
    down = send(down, along_z(-k))
    return send(up, along_z(k)), down


def fill(q_scr, first, own, two, up, down):
    depth = q_scr.shape[1]
    half = depth // 2
    near, next_, last = slice(0, depth), slice(depth, 2 * depth), slice(2 * depth, 2 * depth + half)
    places = (down, next_), (up, near), (own, near), (down, near), (up, next_), (two, next_), None, (two, near)
    for k, place in enumerate(places):
        if place is not None:
            q_scr[first + 16 * k:first + 16 * k + 16, :] = place[0][:, place[1]]
    q_scr[first + 96:first + 112, :half] = up[:, last]
    q_scr[first + 96:first + 112, half:] = down[:, last]


def stage_kernel(own_ref, lab_ref, out_ref, sem):
    copy = pltpu.make_async_copy(own_ref, out_ref, sem)
    copy.start()
    copy.wait()


def stage_call(own, lab):
    return pl.pallas_call(
        stage_kernel,
        in_specs=[hbm(), vmem()],
        out_specs=vmem(),
        out_shape=pltpu.VMEM(own.shape, own.dtype),
        scratch_shapes=[pltpu.SemaphoreType.DMA],
        compiler_params=params(4),
        name="stage",
    )(pltpu.with_memory_space_constraint(own, pltpu.HBM), lab)


def pack_kernel(own_ref, up3_ref, down3_ref, lab_ref, cot_ref, up_ref, down_ref, three_ref, two_ref):
    f32, bf16 = jnp.float32, jnp.bfloat16
    depth = up3_ref.shape[1]
    half = depth // 2
    for ref in (up_ref, down_ref, three_ref, two_ref):
        ref[:, :depth] = own_ref[...]
    up_ref[:, depth:2 * depth] = down3_ref[...]
    up_ref[:, 2 * depth:] = up3_ref[:, :half]
    down_ref[:, depth:2 * depth] = up3_ref[...]
    down_ref[:, 2 * depth:] = down3_ref[:, half:]
    two_ref[:, :depth] = up3_ref[...]
    two_ref[:, depth:] = down3_ref[...]
    label = lab_ref[...]
    high = lax.shift_right_logical(label, 8)
    rest = cot_ref[...]
    terms = [high.astype(f32), (label - high * 256).astype(f32)]
    for _ in range(3):
        term = rest.astype(bf16).astype(f32)
        terms.append(term)
        rest = rest - term
    row = lax.broadcasted_iota(jnp.int32, (16, 128), 0)
    note = jnp.zeros((16, 128), f32)
    for k, term in enumerate(terms):
        note = jnp.where(row == k, term, note)
    three_ref[:, depth:] = note.astype(bf16)


def pack_call(own, up3, down3, lab, cot):
    rows, depth = own.shape
    wide = 2 * depth + depth // 2
    return pl.pallas_call(
        pack_kernel,
        in_specs=[vmem()] * 5,
        out_specs=[vmem()] * 4,
        out_shape=[jax.ShapeDtypeStruct((rows, k), jnp.bfloat16) for k in (wide, wide, depth + 128, 2 * depth)],
        compiler_params=params(4),
        name="pack",
    )(own, up3, down3, lab, cot)


def logits_kernel(scale_ref, shift_ref, own, two, up, down, own_x, two_x, up_x, down_x,
                  mem_ref, lab_ref, valid_ref, e_ref, stat_ref, q_scr, l_scr):
    fill(q_scr, 0, own, two, up, down)
    fill(q_scr, 128, own_x, two_x, up_x, down_x)
    rows, n = l_scr.shape
    scale = scale_ref[0]
    top = jnp.full((rows, 1), NEG, jnp.float32)
    picked = jnp.zeros((rows, 1), jnp.float32)
    for i in range(0, n, BLK):
        raw = lax.dot_general(
            q_scr[...], mem_ref[i:i + BLK, :], (((1,), (1,)), ((), ())), preferred_element_type=jnp.float32
        )
        logit = raw * scale
        column = lax.broadcasted_iota(jnp.int32, logit.shape, 1) + i
        hit = lab_ref[...] == column
        kept = jnp.where(jnp.logical_and(valid_ref[:, i:i + BLK] > 0, jnp.logical_not(hit)), logit, NEG)
        l_scr[:, i:i + BLK] = kept
        top = jnp.maximum(top, jnp.max(kept, axis=1, keepdims=True))
        picked = picked + jnp.sum(jnp.where(hit, logit, 0.0), axis=1, keepdims=True)
    half = rows // 2
    step = 32
    lane = lax.broadcasted_iota(jnp.int32, (step, 128), 1)
    tiles = []
    for r in range(0, rows, step):
        m = top[r:r + step]
        val = l_scr[r:r + step, :]
        e = jnp.exp(val - m)
        e_ref[r:r + step, :] = e.astype(jnp.bfloat16)
        s = jnp.sum(e, axis=1, keepdims=True)
        t = jnp.sum(e * val, axis=1, keepdims=True)
        tiles.append(jnp.where(lane == 0, m, jnp.where(lane == 1, s, jnp.where(lane == 2, t, picked[r:r + step]))))
    full = jnp.concatenate(tiles, axis=0)
    own = pltpu.roll(full[:half].T, shift_ref[0], 1)
    other = pltpu.roll(full[half:].T, shift_ref[0], 1)
    for k in range(4):
        stat_ref[2 * k:2 * k + 1, :] = own[k:k + 1, :]
        stat_ref[2 * k + 1:2 * k + 2, :] = other[k:k + 1, :]


def vmem():
    return pl.BlockSpec(memory_space=pltpu.VMEM)


def smem():
    return pl.BlockSpec(memory_space=pltpu.SMEM)


def params(mib):
    return pltpu.CompilerParams(vmem_limit_bytes=mib * 1024 * 1024)


def logits_call(scale, shift, blocks, memory, lab, valid):
    n, depth = memory.shape
    rows = lab.shape[0]
    return pl.pallas_call(
        logits_kernel,
        in_specs=[smem(), smem()] + [vmem()] * (len(blocks) + 3),
        out_specs=[vmem(), vmem()],
        out_shape=[
            jax.ShapeDtypeStruct((rows, n), jnp.bfloat16),
            jax.ShapeDtypeStruct((8, 128), jnp.float32),
        ],
        scratch_shapes=[
            pltpu.VMEM((rows, depth), jnp.bfloat16),
            pltpu.VMEM((rows, n), jnp.float32),
        ],
        compiler_params=params(8),
        cost_estimate=pl.CostEstimate(
            flops=2 * rows * n * depth, bytes_accessed=2 * n * depth, transcendentals=rows * n
        ),
        name="logits",
    )(scale, shift, *blocks, memory, lab, valid)


FIRST = (3, 0, 6, 1, 4)
SECOND = (2, 5, 7)


def weighted_kernel(e_ref, mem_ref, g_ref, own_ref, first_ref, second_ref):
    second_ref[16 * len(SECOND):, :] = g_ref[...]
    for c in range(0, mem_ref.shape[1], COLS):
        at = slice(c, c + COLS)
        out = jnp.dot(e_ref[...], mem_ref[:, at], preferred_element_type=jnp.float32)
        spread(out, at, own_ref, first_ref, second_ref)


def spread(out, at, own_ref, first_ref, second_ref):
    own_ref[:, at] = out[:128].astype(own_ref.dtype)
    for ref, order in ((first_ref, FIRST), (second_ref, SECOND)):
        for i, k in enumerate(order):
            ref[16 * i:16 * i + 16, at] = out[128 + 16 * k:144 + 16 * k].astype(ref.dtype)


def weighted_call(e, memory, g):
    rows, n = e.shape
    depth = memory.shape[1]
    return pl.pallas_call(
        weighted_kernel,
        in_specs=[vmem()] * 3,
        out_specs=[vmem()] * 3,
        out_shape=[
            jax.ShapeDtypeStruct((128, depth), jnp.float32),
            jax.ShapeDtypeStruct((16 * len(FIRST), depth), jnp.bfloat16),
            jax.ShapeDtypeStruct((32 * len(SECOND), depth), jnp.bfloat16),
        ],
        compiler_params=params(8),
        cost_estimate=pl.CostEstimate(flops=2 * rows * n * depth, bytes_accessed=2 * n * depth, transcendentals=0),
        name="weighted",
    )(e, memory, g)


def labels_kernel(lab_ref, mem_ref, copy_ref, own_ref, first_ref, second_ref, hit_scr, sems):
    rows, n = hit_scr.shape
    pieces = mem_ref.shape[1] // COLS

    def piece(k):
        at = pl.ds(k * COLS, COLS)
        return pltpu.make_async_copy(mem_ref.at[:, at], copy_ref.at[:, at], sems.at[k])

    for k in range(pieces):
        piece(k).start()
    for i in range(0, n, BLK):
        column = lax.broadcasted_iota(jnp.int32, (rows, BLK), 1) + i
        hit_scr[:, i:i + BLK] = jnp.where(lab_ref[...] == column, 1.0, 0.0).astype(jnp.bfloat16)
    for k in range(pieces):
        piece(k).wait()
        at = slice(k * COLS, k * COLS + COLS)
        out = jnp.dot(hit_scr[...], copy_ref[:, at], preferred_element_type=jnp.float32)
        spread(out, at, own_ref, first_ref, second_ref)


def hbm():
    return pl.BlockSpec(memory_space=pltpu.HBM)


def labels_call(lab, memory):
    rows = lab.shape[0]
    n, depth = memory.shape
    return pl.pallas_call(
        labels_kernel,
        in_specs=[vmem(), hbm()],
        out_specs=[vmem()] * 4,
        out_shape=[
            pltpu.VMEM((n, depth), jnp.bfloat16),
            jax.ShapeDtypeStruct((128, depth), jnp.bfloat16),
            jax.ShapeDtypeStruct((16 * len(FIRST), depth), jnp.bfloat16),
            jax.ShapeDtypeStruct((16 * len(SECOND), depth), jnp.bfloat16),
        ],
        scratch_shapes=[pltpu.VMEM((rows, n), jnp.bfloat16), pltpu.SemaphoreType.DMA((depth // COLS,))],
        compiler_params=params(8),
        cost_estimate=pl.CostEstimate(flops=1024, bytes_accessed=1024, transcendentals=0),
        name="label_rows",
    )(lab, pltpu.with_memory_space_constraint(memory, pltpu.HBM))


def merge_kernel(place_ref, cot_ref, up_ref, mid_ref, down_ref, coef_ref, part_ref, sets):
    z, x_lo = place_ref[0], place_ref[1]
    sets[0:3] = up_ref[...]
    sets[3:6] = mid_ref[...]
    sets[6:8] = down_ref[...]
    mine, theirs = sets[4, 0], sets[4, 1]
    flat = []
    for a in range(8):
        at = lax.rem(a - z + 12, 8)
        own, other = sets[at, 0], sets[at, 1]
        row = lax.broadcasted_iota(jnp.int32, other.shape, 0)
        swapped = jnp.where(row % 2 == 0, pltpu.roll(other, 7, 0), pltpu.roll(other, 1, 0))
        is_low = x_lo == 0
        flat += [jnp.where(is_low, own, swapped), jnp.where(is_low, swapped, own)]
    top = flat[0][0:2]
    logit = jnp.zeros_like(top)
    for s in flat:
        top = jnp.maximum(top, s[0:2])
        logit = logit + s[6:8]
    top = jnp.maximum(top, logit)
    rest = jnp.zeros_like(top)
    first = jnp.zeros_like(top)
    for s in flat:
        f = jnp.exp(s[0:2] - top)
        rest = rest + f * s[2:4]
        first = first + f * s[4:6]
    inverse = 1.0 / (rest + jnp.exp(logit - top))
    label_weight = -rest * inverse
    part = jnp.sum(cot_ref[...] * (first * inverse + label_weight * logit), axis=1, keepdims=True)
    part_ref[...] = jnp.broadcast_to(part[0:1] + part[1:2], part_ref.shape)
    c_own = jnp.exp(mine[0:1] - top[0:1]) * inverse[0:1]
    c_other = jnp.exp(theirs[1:2] - top[0:1]) * inverse[0:1]
    row = lax.broadcasted_iota(jnp.int32, (8, 128), 0)
    stack = jnp.where(row == 0, c_own, jnp.where(row == 1, c_other, label_weight[0:1]))
    coef_ref[...] = pltpu.roll(stack, lax.rem((10 - z) * 16, 128), 1).T


def merge_call(place, cot, up, mid, down):
    return pl.pallas_call(
        merge_kernel,
        in_specs=[smem()] + [vmem()] * 4,
        out_specs=[vmem()] * 2,
        out_shape=[jax.ShapeDtypeStruct((128, 8), jnp.float32), jax.ShapeDtypeStruct((8, 128), jnp.float32)],
        scratch_shapes=[pltpu.VMEM((8, 2, 8, 128), jnp.float32)],
        compiler_params=params(4),
        cost_estimate=pl.CostEstimate(flops=5 * 10**9, bytes_accessed=1024, transcendentals=0),
        name="merge",
    )(place, cot, up, mid, down)


def mix_kernel(coef_ref, o_ref, r_ref, g_ref, gr_ref, pu_ref, pd_ref):
    bf16 = jnp.bfloat16
    half = o_ref.shape[1] // 2
    depth = 2 * half
    for i, (ref, first) in enumerate(((pu_ref, 0), (pu_ref, depth), (None, 0), (pd_ref, 0), (pd_ref, depth))):
        p = mixed(coef_ref, o_ref, r_ref, g_ref, gr_ref, FIRST[i], i, i).astype(bf16)
        if i == 2:
            pu_ref[:, 2 * depth:] = p[:, :half]
            pd_ref[:, 2 * depth:] = p[:, half:]
        else:
            ref[:, first:first + depth] = p


def mixed(coef_ref, o_ref, r_ref, g_ref, gr_ref, k, i, j):
    f32 = jnp.float32
    at, there = slice(16 * k, 16 * k + 16), slice(16 * i, 16 * i + 16)
    label = slice(16 * j, 16 * j + 16)
    c = coef_ref[at, :]
    g = g_ref[at, :].astype(f32) + gr_ref[label, :].astype(f32)
    return c[:, 0:1] * o_ref[at, :] + c[:, 1:2] * r_ref[there, :].astype(f32) + c[:, 2:3] * g


def mix_call(coef, o, r, g, gr):
    depth = g.shape[1]
    bf16 = jnp.bfloat16
    return pl.pallas_call(
        mix_kernel,
        in_specs=[vmem()] * 5,
        out_specs=[vmem()] * 2,
        out_shape=[jax.ShapeDtypeStruct((16, 2 * depth + depth // 2), bf16)] * 2,
        compiler_params=params(8),
        name="mix",
    )(coef, o, r, g, gr)


def rest_kernel(coef_ref, o_ref, r_ref, g_ref, *outs):
    for i, out in enumerate(outs):
        out[...] = mixed(coef_ref, o_ref, r_ref, g_ref, r_ref, SECOND[i], i, i + len(SECOND))


def rest_call(coef, o, r, g):
    depth = g.shape[1]
    return pl.pallas_call(
        rest_kernel,
        in_specs=[vmem()] * 4,
        out_specs=[vmem()] * 3,
        out_shape=[jax.ShapeDtypeStruct((16, depth), jnp.float32)] * 3,
        compiler_params=params(8),
        name="rest",
    )(coef, o, r, g)


def final_kernel(count, factor_ref, p0_ref, au_ref, ad_ref, a3_ref, a5_ref, part_ref, out_ref, sum_ref):
    f32 = jnp.float32
    depth = out_ref.shape[1]
    for c in range(0, depth, 512):
        at = slice(c, c + 512)
        near = au_ref[:, at].astype(f32) + ad_ref[:, at].astype(f32)
        wide = a3_ref[:, at].astype(f32) + a5_ref[:, at].astype(f32)
        out_ref[:, at] = (factor_ref[...] * (p0_ref[:, at] + near + wide)).astype(out_ref.dtype)


    total = part_ref[...] / count
    sum_ref[0] = total[0, 0]


def final_call(count, factor, p0, au, ad, a3, a5, part):
    return pl.pallas_call(
        functools.partial(final_kernel, count),
        in_specs=[vmem()] * 7,
        out_specs=[vmem(), smem()],
        out_shape=[jax.ShapeDtypeStruct(a3.shape, a3.dtype), jax.ShapeDtypeStruct((1,), jnp.float32)],
        compiler_params=params(4),
        cost_estimate=pl.CostEstimate(flops=5 * 10**9, bytes_accessed=1024, transcendentals=0),
        name="final",
    )(factor, p0, au, ad, a3, a5, part)


def shards(queries, memory, log_scale, labels, valid, cotangent):
    f32, bf16 = jnp.float32, jnp.bfloat16
    together = lambda *arrays: lax.optimization_barrier(arrays)
    scale = jnp.exp(log_scale)
    where = lax.axis_index("mem")
    z = lax.rem(where, 8)
    x_lo = where // 8
    depth = memory.shape[1]
    half = depth // 2
    start_row = where * memory.shape[0]
    roll_by = lax.rem(z + 6, 8) * 16

    up3, down3 = both(queries, queries, 3)
    own_labels = lax.dynamic_slice_in_dim(labels, x_lo * 128, 128)
    own_cot = lax.dynamic_slice_in_dim(cotangent, x_lo * 128, 128)
    rolled = lax.dynamic_slice_in_dim(jnp.concatenate([own_labels, own_labels]), roll_by, 128)
    staged = stage_call(queries, rolled[None, :])
    up3, staged = together(up3, staged)
    to_up, to_down, to_x, to_x2 = pack_call(staged, up3, down3, rolled[None, :], own_cot[None, :])
    up, down = both(to_up, to_down, 1)
    three_x = send(to_x, PARTNER)
    two_x = send(to_x2, PARTNER)
    up, down, three_x, two_x = together(up, down, three_x, two_x)
    note = three_x[:, depth:].astype(f32)
    lab = (jnp.concatenate([rolled, (note[0] * 256.0 + note[1]).astype(jnp.int32)]) - start_row)[:, None]
    cots = jnp.stack([own_cot, (note[2] + note[3]) + note[4]])
    up_x, down_x = send(up, PARTNER), send(down, PARTNER)
    resident, g, g_first, g_second = labels_call(lab, memory)
    resident = pltpu.with_memory_space_constraint(resident, pltpu.VMEM)
    g_first_x = send(g_first, PARTNER)
    blocks = (to_x, to_x2, up, down, three_x, two_x, up_x, down_x)

    e, stat = logits_call(scale, roll_by.reshape(1), blocks, resident, lab, valid[None, :])
    stat_other = send(stat, PARTNER)
    o, o_first, o_second = weighted_call(e, resident, g_second)
    stat_other, o_first, o_second, g_first_x = together(stat_other, o_first, o_second, g_first_x)
    r_first = send(o_first, PARTNER)
    pair = jnp.stack([stat, stat_other])
    s_up, s_down = both(pair, pair, 1)
    s_up, o_second = together(s_up, o_second)
    three = jnp.stack([s_up, pair, s_down])
    t_up, t_down = both(three, three[:2], 3)
    coef, part = merge_call(jnp.stack([z, x_lo]), cots, t_up, three, t_down)
    r_second = send(o_second, PARTNER)
    pu, pd = mix_call(coef, o, r_first, g, g_first_x)
    au, ad = both(pu, pd, 1)
    p0, p3, p5 = rest_call(coef, o, r_second, g)
    part = (part + send(part, Y2)) + (send(part, Y1) + send(part, Y3))
    au, ad, part, p0, p3, p5 = together(au, ad, part, p0, p3, p5)
    zero = jnp.zeros((16, half), f32)
    near, next_, last = slice(0, depth), slice(depth, 2 * depth), slice(2 * depth, 2 * depth + half)
    p3 = p3 + ad[:, next_].astype(f32) + jnp.concatenate([au[:, last].astype(f32), zero], axis=1)
    p5 = p5 + au[:, next_].astype(f32) + jnp.concatenate([zero, ad[:, last].astype(f32)], axis=1)
    p3, p5, part = together(p3.astype(bf16), p5.astype(bf16), part)
    a3, a5 = both(p3, p5, 3)
    for pairs in (CROSS, CORE):
        part = part + send(part, pairs)
    q_rows = queries.shape[0]
    my_cot = lax.dynamic_slice_in_dim(cotangent, where * q_rows, q_rows)
    count = cotangent.shape[0] * lax.axis_size("dp")
    return final_call(count, (scale * my_cot)[:, None], p0, au, ad, a3, a5, part)


def solution(mesh):
    placed = (P(("dp", "mem"), None), P("mem", None), P(), P("dp"), P("mem"), P("dp"))
    return jax.shard_map(
        shards, mesh=mesh, in_specs=placed, out_specs=(P(("dp", "mem"), None), P()), check_vma=False
    )
```

```python
import functools

import jax
import jax.numpy as jnp
from jax import lax
from jax.experimental import pallas as pl
from jax.experimental.pallas import tpu as pltpu
from jax.sharding import PartitionSpec as P

AXES = ("dp", "mem")
NEG = -1e30
BLK = 512
COLS = 1024


def table(move):
    pairs = []
    for y in range(4):
        for x in range(4):
            for c in range(2):
                for z in range(8):
                    index = lambda y, x, c, z: (((y * 2 + x // 2) * 2 + c) * 2 + x % 2) * 8 + z
                    pairs.append((index(y, x, c, z), index(*move(y, x, c, z))))
    return pairs


def along_z(k):
    return table(lambda y, x, c, z: (y, x, c, (z + k) % 8))


def partner_of(x, c):
    if c == 0:
        return x ^ 1
    return (x + 1) % 4 if x % 2 else (x - 1) % 4


PARTNER = table(lambda y, x, c, z: (y, partner_of(x, c), c, z))
CORE = table(lambda y, x, c, z: (y, x, 1 - c, z))
CROSS = table(lambda y, x, c, z: (y, partner_of(x, 1 - c), c, z))
Y1 = table(lambda y, x, c, z: (y ^ 1, x, c, z))
Y3 = table(lambda y, x, c, z: (y ^ 3, x, c, z))
Y2 = table(lambda y, x, c, z: (y ^ 2, x, c, z))


def send(x, pairs):
    return lax.ppermute(x, AXES, pairs)


def both(up, down, k):
    down = send(down, along_z(-k))
    return send(up, along_z(k)), down


def fill(q_scr, first, own, two, up, down):
    depth = q_scr.shape[1]
    half = depth // 2
    near, next_, last = slice(0, depth), slice(depth, 2 * depth), slice(2 * depth, 2 * depth + half)
    places = (down, next_), (up, near), (own, near), (down, near), (up, next_), (two, next_), None, (two, near)
    for k, place in enumerate(places):
        if place is not None:
            q_scr[first + 16 * k:first + 16 * k + 16, :] = place[0][:, place[1]]
    q_scr[first + 96:first + 112, :half] = up[:, last]
    q_scr[first + 96:first + 112, half:] = down[:, last]


def stage_kernel(own_ref, lab_ref, out_ref, sem):
    copy = pltpu.make_async_copy(own_ref, out_ref, sem)
    copy.start()
    copy.wait()


def stage_call(own, lab):
    return pl.pallas_call(
        stage_kernel,
        in_specs=[hbm(), vmem()],
        out_specs=vmem(),
        out_shape=pltpu.VMEM(own.shape, own.dtype),
        scratch_shapes=[pltpu.SemaphoreType.DMA],
        compiler_params=params(4),
        name="stage",
    )(pltpu.with_memory_space_constraint(own, pltpu.HBM), lab)


def pack_kernel(own_ref, up3_ref, down3_ref, lab_ref, cot_ref, up_ref, down_ref, three_ref, two_ref):
    f32, bf16 = jnp.float32, jnp.bfloat16
    depth = up3_ref.shape[1]
    half = depth // 2
    for ref in (up_ref, down_ref, three_ref, two_ref):
        ref[:, :depth] = own_ref[...]
    up_ref[:, depth:2 * depth] = down3_ref[...]
    up_ref[:, 2 * depth:] = up3_ref[:, :half]
    down_ref[:, depth:2 * depth] = up3_ref[...]
    down_ref[:, 2 * depth:] = down3_ref[:, half:]
    two_ref[:, :depth] = up3_ref[...]
    two_ref[:, depth:] = down3_ref[...]
    label = lab_ref[...]
    high = lax.shift_right_logical(label, 8)
    rest = cot_ref[...]
    terms = [high.astype(f32), (label - high * 256).astype(f32)]
    for _ in range(3):
        term = rest.astype(bf16).astype(f32)
        terms.append(term)
        rest = rest - term
    row = lax.broadcasted_iota(jnp.int32, (16, 128), 0)
    note = jnp.zeros((16, 128), f32)
    for k, term in enumerate(terms):
        note = jnp.where(row == k, term, note)
    three_ref[:, depth:] = note.astype(bf16)


def pack_call(own, up3, down3, lab, cot):
    rows, depth = own.shape
    wide = 2 * depth + depth // 2
    return pl.pallas_call(
        pack_kernel,
        in_specs=[vmem()] * 5,
        out_specs=[vmem()] * 4,
        out_shape=[jax.ShapeDtypeStruct((rows, k), jnp.bfloat16) for k in (wide, wide, depth + 128, 2 * depth)],
        compiler_params=params(4),
        name="pack",
    )(own, up3, down3, lab, cot)


def logits_kernel(scale_ref, shift_ref, own, two, up, down, own_x, two_x, up_x, down_x,
                  mem_ref, lab_ref, valid_ref, e_ref, stat_ref, q_scr, l_scr):
    fill(q_scr, 0, own, two, up, down)
    fill(q_scr, 128, own_x, two_x, up_x, down_x)
    rows, n = l_scr.shape
    scale = scale_ref[0]
    top = jnp.full((rows, 1), NEG, jnp.float32)
    picked = jnp.zeros((rows, 1), jnp.float32)
    for i in range(0, n, BLK):
        raw = lax.dot_general(
            q_scr[...], mem_ref[i:i + BLK, :], (((1,), (1,)), ((), ())), preferred_element_type=jnp.float32
        )
        logit = raw * scale
        column = lax.broadcasted_iota(jnp.int32, logit.shape, 1) + i
        hit = lab_ref[...] == column
        kept = jnp.where(jnp.logical_and(valid_ref[:, i:i + BLK] > 0, jnp.logical_not(hit)), logit, NEG)
        l_scr[:, i:i + BLK] = kept
        top = jnp.maximum(top, jnp.max(kept, axis=1, keepdims=True))
        picked = picked + jnp.sum(jnp.where(hit, logit, 0.0), axis=1, keepdims=True)
    half = rows // 2
    step = 32
    lane = lax.broadcasted_iota(jnp.int32, (step, 128), 1)
    tiles = []
    for r in range(0, rows, step):
        m = top[r:r + step]
        val = l_scr[r:r + step, :]
        e = jnp.exp(val - m)
        e_ref[r:r + step, :] = e.astype(jnp.bfloat16)
        s = jnp.sum(e, axis=1, keepdims=True)
        t = jnp.sum(e * val, axis=1, keepdims=True)
        tiles.append(jnp.where(lane == 0, m, jnp.where(lane == 1, s, jnp.where(lane == 2, t, picked[r:r + step]))))
    full = jnp.concatenate(tiles, axis=0)
    own = pltpu.roll(full[:half].T, shift_ref[0], 1)
    other = pltpu.roll(full[half:].T, shift_ref[0], 1)
    for k in range(4):
        stat_ref[2 * k:2 * k + 1, :] = own[k:k + 1, :]
        stat_ref[2 * k + 1:2 * k + 2, :] = other[k:k + 1, :]


def vmem():
    return pl.BlockSpec(memory_space=pltpu.VMEM)


def smem():
    return pl.BlockSpec(memory_space=pltpu.SMEM)


def params(mib):
    return pltpu.CompilerParams(vmem_limit_bytes=mib * 1024 * 1024)


def logits_call(scale, shift, blocks, memory, lab, valid):
    n, depth = memory.shape
    rows = lab.shape[0]
    return pl.pallas_call(
        logits_kernel,
        in_specs=[smem(), smem()] + [vmem()] * (len(blocks) + 3),
        out_specs=[vmem(), vmem()],
        out_shape=[
            jax.ShapeDtypeStruct((rows, n), jnp.bfloat16),
            jax.ShapeDtypeStruct((8, 128), jnp.float32),
        ],
        scratch_shapes=[
            pltpu.VMEM((rows, depth), jnp.bfloat16),
            pltpu.VMEM((rows, n), jnp.float32),
        ],
        compiler_params=params(8),
        cost_estimate=pl.CostEstimate(
            flops=2 * rows * n * depth, bytes_accessed=2 * n * depth, transcendentals=rows * n
        ),
        name="logits",
    )(scale, shift, *blocks, memory, lab, valid)


FIRST = (3, 0, 6, 1, 4)
SECOND = (2, 5, 7)


def weighted_kernel(e_ref, mem_ref, g_ref, own_ref, first_ref, second_ref):
    second_ref[16 * len(SECOND):, :] = g_ref[...]
    for c in range(0, mem_ref.shape[1], COLS):
        at = slice(c, c + COLS)
        out = jnp.dot(e_ref[...], mem_ref[:, at], preferred_element_type=jnp.float32)
        spread(out, at, own_ref, first_ref, second_ref)


def spread(out, at, own_ref, first_ref, second_ref):
    own_ref[:, at] = out[:128].astype(own_ref.dtype)
    for ref, order in ((first_ref, FIRST), (second_ref, SECOND)):
        for i, k in enumerate(order):
            ref[16 * i:16 * i + 16, at] = out[128 + 16 * k:144 + 16 * k].astype(ref.dtype)


def weighted_call(e, memory, g):
    rows, n = e.shape
    depth = memory.shape[1]
    return pl.pallas_call(
        weighted_kernel,
        in_specs=[vmem()] * 3,
        out_specs=[vmem()] * 3,
        out_shape=[
            jax.ShapeDtypeStruct((128, depth), jnp.float32),
            jax.ShapeDtypeStruct((16 * len(FIRST), depth), jnp.bfloat16),
            jax.ShapeDtypeStruct((32 * len(SECOND), depth), jnp.bfloat16),
        ],
        compiler_params=params(8),
        cost_estimate=pl.CostEstimate(flops=2 * rows * n * depth, bytes_accessed=2 * n * depth, transcendentals=0),
        name="weighted",
    )(e, memory, g)


def labels_kernel(lab_ref, mem_ref, copy_ref, own_ref, first_ref, second_ref, hit_scr, sems):
    rows, n = hit_scr.shape
    pieces = mem_ref.shape[1] // COLS

    def piece(k):
        at = pl.ds(k * COLS, COLS)
        return pltpu.make_async_copy(mem_ref.at[:, at], copy_ref.at[:, at], sems.at[k])

    for k in range(pieces):
        piece(k).start()
    for i in range(0, n, BLK):
        column = lax.broadcasted_iota(jnp.int32, (rows, BLK), 1) + i
        hit_scr[:, i:i + BLK] = jnp.where(lab_ref[...] == column, 1.0, 0.0).astype(jnp.bfloat16)
    for k in range(pieces):
        piece(k).wait()
        at = slice(k * COLS, k * COLS + COLS)
        out = jnp.dot(hit_scr[...], copy_ref[:, at], preferred_element_type=jnp.float32)
        spread(out, at, own_ref, first_ref, second_ref)


def hbm():
    return pl.BlockSpec(memory_space=pltpu.HBM)


def labels_call(lab, memory):
    rows = lab.shape[0]
    n, depth = memory.shape
    return pl.pallas_call(
        labels_kernel,
        in_specs=[vmem(), hbm()],
        out_specs=[vmem()] * 4,
        out_shape=[
            pltpu.VMEM((n, depth), jnp.bfloat16),
            jax.ShapeDtypeStruct((128, depth), jnp.bfloat16),
            jax.ShapeDtypeStruct((16 * len(FIRST), depth), jnp.bfloat16),
            jax.ShapeDtypeStruct((16 * len(SECOND), depth), jnp.bfloat16),
        ],
        scratch_shapes=[pltpu.VMEM((rows, n), jnp.bfloat16), pltpu.SemaphoreType.DMA((depth // COLS,))],
        compiler_params=params(8),
        cost_estimate=pl.CostEstimate(flops=1024, bytes_accessed=1024, transcendentals=0),
        name="label_rows",
    )(lab, pltpu.with_memory_space_constraint(memory, pltpu.HBM))


def merge_kernel(place_ref, cot_ref, up_ref, mid_ref, down_ref, coef_ref, part_ref, sets):
    z, x_lo = place_ref[0], place_ref[1]
    sets[0:3] = up_ref[...]
    sets[3:6] = mid_ref[...]
    sets[6:8] = down_ref[...]
    mine, theirs = sets[4, 0], sets[4, 1]
    flat = []
    for a in range(8):
        at = lax.rem(a - z + 12, 8)
        own, other = sets[at, 0], sets[at, 1]
        row = lax.broadcasted_iota(jnp.int32, other.shape, 0)
        swapped = jnp.where(row % 2 == 0, pltpu.roll(other, 7, 0), pltpu.roll(other, 1, 0))
        is_low = x_lo == 0
        flat += [jnp.where(is_low, own, swapped), jnp.where(is_low, swapped, own)]
    top = flat[0][0:2]
    logit = jnp.zeros_like(top)
    for s in flat:
        top = jnp.maximum(top, s[0:2])
        logit = logit + s[6:8]
    top = jnp.maximum(top, logit)
    rest = jnp.zeros_like(top)
    first = jnp.zeros_like(top)
    for s in flat:
        f = jnp.exp(s[0:2] - top)
        rest = rest + f * s[2:4]
        first = first + f * s[4:6]
    inverse = 1.0 / (rest + jnp.exp(logit - top))
    label_weight = -rest * inverse
    part = jnp.sum(cot_ref[...] * (first * inverse + label_weight * logit), axis=1, keepdims=True)
    part_ref[...] = jnp.broadcast_to(part[0:1] + part[1:2], part_ref.shape)
    c_own = jnp.exp(mine[0:1] - top[0:1]) * inverse[0:1]
    c_other = jnp.exp(theirs[1:2] - top[0:1]) * inverse[0:1]
    row = lax.broadcasted_iota(jnp.int32, (8, 128), 0)
    stack = jnp.where(row == 0, c_own, jnp.where(row == 1, c_other, label_weight[0:1]))
    coef_ref[...] = pltpu.roll(stack, lax.rem((10 - z) * 16, 128), 1).T


def merge_call(place, cot, up, mid, down):
    return pl.pallas_call(
        merge_kernel,
        in_specs=[smem()] + [vmem()] * 4,
        out_specs=[vmem()] * 2,
        out_shape=[jax.ShapeDtypeStruct((128, 8), jnp.float32), jax.ShapeDtypeStruct((8, 128), jnp.float32)],
        scratch_shapes=[pltpu.VMEM((8, 2, 8, 128), jnp.float32)],
        compiler_params=params(4),
        cost_estimate=pl.CostEstimate(flops=5 * 10**9, bytes_accessed=1024, transcendentals=0),
        name="merge",
    )(place, cot, up, mid, down)


def mix_kernel(coef_ref, o_ref, r_ref, g_ref, gr_ref, pu_ref, pd_ref):
    bf16 = jnp.bfloat16
    half = o_ref.shape[1] // 2
    depth = 2 * half
    for i, (ref, first) in enumerate(((pu_ref, 0), (pu_ref, depth), (None, 0), (pd_ref, 0), (pd_ref, depth))):
        p = mixed(coef_ref, o_ref, r_ref, g_ref, gr_ref, FIRST[i], i, i).astype(bf16)
        if i == 2:
            pu_ref[:, 2 * depth:] = p[:, :half]
            pd_ref[:, 2 * depth:] = p[:, half:]
        else:
            ref[:, first:first + depth] = p


def mixed(coef_ref, o_ref, r_ref, g_ref, gr_ref, k, i, j):
    f32 = jnp.float32
    at, there = slice(16 * k, 16 * k + 16), slice(16 * i, 16 * i + 16)
    label = slice(16 * j, 16 * j + 16)
    c = coef_ref[at, :]
    g = g_ref[at, :].astype(f32) + gr_ref[label, :].astype(f32)
    return c[:, 0:1] * o_ref[at, :] + c[:, 1:2] * r_ref[there, :].astype(f32) + c[:, 2:3] * g


def mix_call(coef, o, r, g, gr):
    depth = g.shape[1]
    bf16 = jnp.bfloat16
    return pl.pallas_call(
        mix_kernel,
        in_specs=[vmem()] * 5,
        out_specs=[vmem()] * 2,
        out_shape=[jax.ShapeDtypeStruct((16, 2 * depth + depth // 2), bf16)] * 2,
        compiler_params=params(8),
        name="mix",
    )(coef, o, r, g, gr)


def rest_kernel(coef_ref, o_ref, r_ref, g_ref, *outs):
    for i, out in enumerate(outs):
        out[...] = mixed(coef_ref, o_ref, r_ref, g_ref, r_ref, SECOND[i], i, i + len(SECOND))


def rest_call(coef, o, r, g):
    depth = g.shape[1]
    return pl.pallas_call(
        rest_kernel,
        in_specs=[vmem()] * 4,
        out_specs=[vmem()] * 3,
        out_shape=[jax.ShapeDtypeStruct((16, depth), jnp.float32)] * 3,
        compiler_params=params(8),
        name="rest",
    )(coef, o, r, g)


def final_kernel(count, factor_ref, p0_ref, au_ref, ad_ref, a3_ref, a5_ref, part_ref, out_ref, sum_ref):
    f32 = jnp.float32
    depth = out_ref.shape[1]
    for c in range(0, depth, 512):
        at = slice(c, c + 512)
        near = au_ref[:, at].astype(f32) + ad_ref[:, at].astype(f32)
        wide = a3_ref[:, at].astype(f32) + a5_ref[:, at].astype(f32)
        out_ref[:, at] = (factor_ref[...] * (p0_ref[:, at] + near + wide)).astype(out_ref.dtype)


    total = part_ref[...] / count
    sum_ref[0] = total[0, 0]


def final_call(count, factor, p0, au, ad, a3, a5, part):
    return pl.pallas_call(
        functools.partial(final_kernel, count),
        in_specs=[vmem()] * 7,
        out_specs=[vmem(), smem()],
        out_shape=[jax.ShapeDtypeStruct(a3.shape, a3.dtype), jax.ShapeDtypeStruct((1,), jnp.float32)],
        compiler_params=params(4),
        cost_estimate=pl.CostEstimate(flops=5 * 10**9, bytes_accessed=1024, transcendentals=0),
        name="final",
    )(factor, p0, au, ad, a3, a5, part)


def shards(queries, memory, log_scale, labels, valid, cotangent):
    f32, bf16 = jnp.float32, jnp.bfloat16
    together = lambda *arrays: lax.optimization_barrier(arrays)
    scale = jnp.exp(log_scale)
    where = lax.axis_index("mem")
    z = lax.rem(where, 8)
    x_lo = where // 8
    depth = memory.shape[1]
    half = depth // 2
    start_row = where * memory.shape[0]
    roll_by = lax.rem(z + 6, 8) * 16

    up3, down3 = both(queries, queries, 3)
    own_labels = lax.dynamic_slice_in_dim(labels, x_lo * 128, 128)
    own_cot = lax.dynamic_slice_in_dim(cotangent, x_lo * 128, 128)
    rolled = lax.dynamic_slice_in_dim(jnp.concatenate([own_labels, own_labels]), roll_by, 128)
    staged = stage_call(queries, rolled[None, :])
    up3, staged = together(up3, staged)
    to_up, to_down, to_x, to_x2 = pack_call(staged, up3, down3, rolled[None, :], own_cot[None, :])
    up, down = both(to_up, to_down, 1)
    three_x = send(to_x, PARTNER)
    two_x = send(to_x2, PARTNER)
    up, down, three_x, two_x = together(up, down, three_x, two_x)
    note = three_x[:, depth:].astype(f32)
    lab = (jnp.concatenate([rolled, (note[0] * 256.0 + note[1]).astype(jnp.int32)]) - start_row)[:, None]
    cots = jnp.stack([own_cot, (note[2] + note[3]) + note[4]])
    up_x, down_x = send(up, PARTNER), send(down, PARTNER)
    resident, g, g_first, g_second = labels_call(lab, memory)
    resident = pltpu.with_memory_space_constraint(resident, pltpu.VMEM)
    g_first_x = send(g_first, PARTNER)
    blocks = (to_x, to_x2, up, down, three_x, two_x, up_x, down_x)

    e, stat = logits_call(scale, roll_by.reshape(1), blocks, resident, lab, valid[None, :])
    stat_other = send(stat, PARTNER)
    o, o_first, o_second = weighted_call(e, resident, g_second)
    stat_other, o_first, o_second, g_first_x = together(stat_other, o_first, o_second, g_first_x)
    r_first = send(o_first, PARTNER)
    pair = jnp.stack([stat, stat_other])
    s_up, s_down = both(pair, pair, 1)
    s_up, o_second = together(s_up, o_second)
    three = jnp.stack([s_up, pair, s_down])
    t_up, t_down = both(three, three[:2], 3)
    coef, part = merge_call(jnp.stack([z, x_lo]), cots, t_up, three, t_down)
    r_second = send(o_second, PARTNER)
    pu, pd = mix_call(coef, o, r_first, g, g_first_x)
    au, ad = both(pu, pd, 1)
    p0, p3, p5 = rest_call(coef, o, r_second, g)
    part = (part + send(part, Y2)) + (send(part, Y1) + send(part, Y3))
    au, ad, p0, p3, p5 = together(au, ad, p0, p3, p5)
    zero = jnp.zeros((16, half), f32)
    near, next_, last = slice(0, depth), slice(depth, 2 * depth), slice(2 * depth, 2 * depth + half)
    p3 = p3 + ad[:, next_].astype(f32) + jnp.concatenate([au[:, last].astype(f32), zero], axis=1)
    p5 = p5 + au[:, next_].astype(f32) + jnp.concatenate([zero, ad[:, last].astype(f32)], axis=1)
    p3, p5 = together(p3.astype(bf16), p5.astype(bf16))
    a3, a5 = both(p3, p5, 3)
    for pairs in (CROSS, CORE):
        part = part + send(part, pairs)
    q_rows = queries.shape[0]
    my_cot = lax.dynamic_slice_in_dim(cotangent, where * q_rows, q_rows)
    count = cotangent.shape[0] * lax.axis_size("dp")
    return final_call(count, (scale * my_cot)[:, None], p0, au, ad, a3, a5, part)


def solution(mesh):
    placed = (P(("dp", "mem"), None), P("mem", None), P(), P("dp"), P("mem"), P("dp"))
    return jax.shard_map(
        shards, mesh=mesh, in_specs=placed, out_specs=(P(("dp", "mem"), None), P()), check_vma=False
    )
```
